256 devices in a mesh: dp: 16 (over x, y), sp: 16 (over z, core).
Axes of the slice: x: 4, y: 4, z: 8, core: 2. Of those that a mesh axis runs over, the one named last changes fastest.
Arguments:
- hidden: bfloat16 [256, 128, 2048], P(('dp', 'sp')), may hold values from -6 to 6
- lengths: int32 [256], P('dp'), may hold values from 32 to 128, as said below
- source_slot: int32 [256], replicated, may hold values from 0 to 255, as said below
- old_state: float32 [256, 16, 2, 128, 128], P('dp', 'sp'), may hold values from -6 to 6
- old_conv: bfloat16 [256, 16, 3, 512], P('dp', 'sp'), may hold values from -6 to 6
- w_in: bfloat16 [2048, 16, 768], P(None, 'sp'), may hold values from -0.125 to 0.125
- w_gates: bfloat16 [2048, 16, 4], P(None, 'sp'), may hold values from -0.125 to 0.125
- conv_weight: float32 [16, 4, 512], P('sp'), may hold values from -3 to 3
- decay_scale: float32 [16, 2], P('sp'), may hold values from 0.001 to 0.06
- dt_bias: float32 [16, 2], P('sp'), may hold values from -1 to 1
- norm_gain: float32 [128], replicated, may hold values from 0.5 to 1.5
- w_out: bfloat16 [16, 256, 2048], P('sp'), may hold values from -0.09375 to 0.09375
Outputs:
- layer_out: bfloat16 [256, 128, 2048], P(('dp', 'sp'))
- new_state: float32 [256, 16, 2, 128, 128], P('dp', 'sp')
- new_conv: bfloat16 [256, 16, 3, 512], P('dp', 'sp')
The draws below stay inside these ranges and needn't reach their ends.
Inputs may be any that keep to these rules, and one draw needn't show every extreme that they name: A permutation of the 256 slots: new slot r takes the states held at old slot source_slot[r]. Old slot o lies with dp index o // 16, new slot r with r // 16. The 16 old slots of each dp index go to exactly half of the dp indices, 2 to each of them. `lengths`: some rollout has exactly 128 live tokens.
All inputs are finite; a program needn't handle non-finite values.
Results may differ from the reference program's by a relative error of at most 0.007.
Values may be sent and summed in bfloat16 or wider, within the bound.
No kernel may reach another device: no remote copies, remote signals or barrier semaphores. Data moves between devices by JAX's collectives and lax.ppermute only.
A program may use at most 128 MiB of HBM per device.

```python
import math
import jax
import jax.numpy as jnp
from jax import lax

D = 2048
QK_HEADS = 16
DK = 128
DV = 128
V_PER = 2
K_CONV = 4
R_DEV = 16
LEN = 128
ROLLOUTS = 256
CONV = 512
PAIR = 2
N_DP = 16


def draw_source_slot(key, part):
    key = jax.random.fold_in(key, 17)
    shift_key, owner_key, order_key, slot_key = jax.random.split(key, 4)
    distinct_shifts = jax.random.permutation(shift_key, N_DP)[:R_DEV // PAIR]
    shift_list = jnp.repeat(distinct_shifts, PAIR)

    def shuffle_row(row_key):
        return jax.random.permutation(row_key, shift_list)
    row_keys = jax.random.split(order_key, N_DP)
    shifts = jax.vmap(shuffle_row)(row_keys)
    relabel = jax.random.permutation(owner_key, N_DP)
    old_owner = jnp.arange(N_DP, dtype=jnp.int32)[:, None]
    target = relabel[(old_owner + shifts) % N_DP].reshape(-1)
    sort_score = target * ROLLOUTS + jax.random.permutation(slot_key, ROLLOUTS)
    return jnp.argsort(sort_score).astype(jnp.int32)


def draw_lengths(key, part):
    key = jax.random.fold_in(key, 5)
    value_key, index_key = jax.random.split(key)
    length_vals = jax.random.randint(value_key, (ROLLOUTS,), LEN // 4, LEN + 1)
    full_index = jax.random.randint(index_key, (), 0, ROLLOUTS)
    return length_vals.at[full_index].set(LEN).astype(jnp.int32)


def level_of(rng, dims, shards, smallest, largest):
    def one(position, blocks):
        draws = jax.random.uniform(jax.random.fold_in(jax.random.fold_in(rng, 6), position), (blocks,), jnp.float32, smallest / len(shards), largest / len(shards))
        return jnp.repeat(jnp.exp(draws), dims[position] // blocks).reshape((-1,) + (1,) * (len(dims) - position - 1))

    gain = one(*shards[0])
    for cut in shards[1:]:
        gain = gain * one(*cut)
    return gain


def normal_values(rng, dims, scale, limit, cuts=(), held_as=jnp.bfloat16):
    entries = jax.random.normal(rng, dims, jnp.float32) * scale
    if len(cuts) > 0:
        entries = level_of(rng, dims, cuts, -0.22, 0.18) * entries
    return jnp.clip(entries, min=-limit, max=limit).astype(held_as)


def setup_inputs(seed: int = 0) -> dict:
    seeds = jax.random.split(jax.random.key(seed), 13)
    hidden = normal_values(seeds[0], (ROLLOUTS, LEN, D), 1.0, 6.0, ((0, 256),))
    lengths = draw_lengths(jax.random.fold_in(seeds[12], 71), 0)
    source_slot = draw_source_slot(jax.random.fold_in(seeds[12], 71), 0)
    old_state = normal_values(seeds[3], (ROLLOUTS, QK_HEADS, V_PER, DK, DV), 1.0, 6.0, ((0, 16), (1, 16)), jnp.float32)
    old_conv = normal_values(seeds[4], (ROLLOUTS, QK_HEADS, K_CONV - 1, CONV), 1.0, 6.0, ((0, 16), (1, 16)))
    w_in = normal_values(seeds[5], (D, QK_HEADS, CONV + V_PER * DV), D ** -0.5, 0.125, ((1, 16),))
    w_gates = normal_values(seeds[6], (D, QK_HEADS, 2 * V_PER), D ** -0.5, 0.125, ((1, 16),))
    conv_weight = normal_values(seeds[7], (QK_HEADS, K_CONV, CONV), K_CONV ** -0.5, 3.0, ((0, 16),), jnp.float32)
    decay_scale = jnp.clip(jnp.exp(math.log(0.06) - 4.0943445 * jax.random.uniform(seeds[8], (QK_HEADS, V_PER), jnp.float32) ** level_of(seeds[8], (QK_HEADS, V_PER), ((0, 16),), -0.2, 0.2)), 0.001, 0.06)
    dt_bias = jnp.clip(jax.random.uniform(seeds[9], (QK_HEADS, V_PER), jnp.float32, -1.0, 1.0) * level_of(seeds[9], (QK_HEADS, V_PER), ((0, 16),), -0.4, 0.0), -1.0, 1.0)
    norm_gain = jnp.clip(1.0 + 0.1 * jax.random.normal(seeds[10], (DV,), jnp.float32), 0.5, 1.5)
    w_out = normal_values(seeds[11], (QK_HEADS, V_PER * DV, D), (QK_HEADS * V_PER * DV) ** -0.5, 0.09375, ((0, 16),))
    return dict(hidden=hidden, lengths=lengths, source_slot=source_slot, old_state=old_state, old_conv=old_conv, w_in=w_in, w_gates=w_gates, conv_weight=conv_weight, decay_scale=decay_scale, dt_bias=dt_bias, norm_gain=norm_gain, w_out=w_out)


HIGHEST = lax.Precision.HIGHEST

def unit_rows(values):
    return values * lax.rsqrt(lax.optimization_barrier(jnp.sum(values * values, axis=-1, keepdims=True)) + 1e-06)

def rms_gate(values, gate_vec, gain_vec):
    inv_rms = lax.rsqrt(lax.optimization_barrier(jnp.mean(values * values, axis=-1, keepdims=True)) + 1e-06)
    return values * inv_rms * gain_vec * jax.nn.silu(gate_vec)

def reference(hidden, lengths, source_slot, old_state, old_conv, w_in, w_gates, conv_weight, decay_scale, dt_bias, norm_gain, w_out):
    state_start = old_state[source_slot]
    conv_start = old_conv[source_slot]
    flat_in = w_in.reshape(D, QK_HEADS * (CONV + V_PER * DV))
    flat_gates = w_gates.reshape(D, QK_HEADS * 2 * V_PER)
    flat_out = w_out.reshape(QK_HEADS * V_PER * DV, D)
    positions = jnp.arange(LEN, dtype=jnp.int32)

    def one_rollout(packed):
        rollout_rows, length, delta_state, conv_state = packed
        mixed_proj = jnp.dot(rollout_rows, flat_in, preferred_element_type=jnp.float32).astype(jnp.bfloat16)
        mixed_proj = mixed_proj.reshape(LEN, QK_HEADS, CONV + V_PER * DV)
        gate_proj = jnp.dot(rollout_rows, flat_gates, preferred_element_type=jnp.float32).reshape(LEN, QK_HEADS, 2 * V_PER)
        conv_seq = jnp.concatenate([jnp.transpose(conv_state, (1, 0, 2)), mixed_proj[:, :, :CONV]], axis=0)
        conv_out = jnp.zeros((LEN, QK_HEADS, CONV), jnp.float32)
        for tap in range(K_CONV):
            conv_out = conv_out + conv_weight[:, tap, :] * conv_seq[tap:tap + LEN].astype(jnp.float32)
        activated = jax.nn.silu(conv_out)
        conv_next = jnp.transpose(lax.dynamic_slice_in_dim(conv_seq, length.astype(jnp.int32), K_CONV - 1, 0), (1, 0, 2))
        query_rows = unit_rows(activated[..., :DK]) * DK ** (-0.5)
        key_rows = unit_rows(activated[..., DK:2 * DK])
        value_rows = activated[..., 2 * DK:].reshape(LEN, QK_HEADS, V_PER, DV)
        live = (positions < length).astype(jnp.float32)[:, None, None]
        beta_rows = jax.nn.sigmoid(gate_proj[..., :V_PER]) * live
        decay_rows = -decay_scale * jax.nn.softplus(gate_proj[..., V_PER:] + dt_bias) * live

        def token_step(carry_state, token):
            query_t, key_t, value_t, beta_t, decay_t = token
            carry_state = jnp.exp(decay_t)[..., None, None] * carry_state
            predicted = jnp.einsum('hk,hjkd->hjd', key_t, carry_state, precision=HIGHEST)
            written = beta_t[..., None] * (value_t - predicted)
            carry_state = carry_state + key_t[:, None, :, None] * written[:, :, None, :]
            read_out = jnp.einsum('hk,hjkd->hjd', query_t, carry_state, precision=HIGHEST)
            return (carry_state, read_out)
        final_state, read_all = lax.scan(token_step, delta_state, (query_rows, key_rows, value_rows, beta_rows, decay_rows))
        gate_z = mixed_proj[..., CONV:].reshape(LEN, QK_HEADS, V_PER, DV).astype(jnp.float32)
        gated = rms_gate(read_all, gate_z, norm_gain) * live[..., None]
        core_rows = gated.astype(jnp.bfloat16).reshape(LEN, QK_HEADS * V_PER * DV)
        out_rows = jnp.dot(core_rows, flat_out, preferred_element_type=jnp.float32).astype(jnp.bfloat16)
        return (out_rows, final_state, conv_next)
    layer_out, new_state, new_conv = lax.map(one_rollout, (hidden, lengths, state_start, conv_start))
    return (layer_out, new_state, new_conv)
```

```python
import functools

import jax
import jax.numpy as jnp
from jax import lax
from jax.experimental import pallas as pl
from jax.experimental.pallas import tpu as pltpu
from jax.sharding import PartitionSpec as P

F32 = jnp.float32
BF16 = jnp.bfloat16
LEN = 128
DK = 128
DV = 128
CONV = 512
SLOTS = 32
SLOT_ROWS = 272
SMEM = pl.BlockSpec(memory_space=pltpu.SMEM)
VMEM = pl.BlockSpec(memory_space=pltpu.VMEM)
ANY = pl.BlockSpec(memory_space=pl.ANY)


def dot(lhs, rhs):
    return jnp.dot(lhs, rhs, preferred_element_type=F32)


def pack_kernel(info_ref, source_ref, state_ref, conv_ref, out_ref, src_scr):
    me = info_ref[0]

    def one_target(target, _):
        found = jnp.int32(0)
        for i in range(16):
            value = source_ref[target * 16 + i]
            src_scr[target * 2 + found] = value & 15
            found = found + jnp.where((value >> 4) == me, 1, 0)
        return 0

    lax.fori_loop(0, 16, one_target, 0)

    def one_slot(slot, _):
        src = src_scr[slot] & 15
        for j in range(2):
            out_ref[slot, j * 128 : (j + 1) * 128, :] = state_ref[src, j].astype(BF16)
        out_ref[slot, 256:272, :] = conv_ref[src]
        return 0

    lax.fori_loop(0, SLOTS, one_slot, 0)


def delta_kernel(
    count,
    first,
    has_alias,
    ids_ref,
    source_ref,
    lengths_ref,
    w_ref,
    wg_ref,
    convw_ref,
    gvec_ref,
    arrived_ref,
    *refs,
):
    x_refs = refs[:count]
    refs = refs[count:]
    if has_alias:
        refs = refs[2:]
    core_refs = refs[: count // 2]
    state_ref, tail_ref = refs[count // 2 : count // 2 + 2]
    start_scr, seq_scr, z_scr, gate_scr, state_scr, tail_scr, in_sem, out_sem, tail_sem = refs[
        count // 2 + 2 :
    ]
    me = ids_ref[16]
    rollouts = [ids_ref[first + i] for i in range(count)]
    lens = [lengths_ref[r] for r in rollouts]

    in_copies = []
    for i, r in enumerate(rollouts):
        owner = source_ref[me * 16 + r] >> 4
        rank = jnp.int32(0)
        for k in range(16):
            same = (source_ref[me * 16 + k] >> 4) == owner
            rank = rank + jnp.where(same & (k < r), 1, 0)
        slot = jnp.minimum(owner * 2 + rank, SLOTS - 1)
        copy = pltpu.make_async_copy(arrived_ref.at[slot], start_scr.at[i], in_sem.at[i])
        copy.start()
        in_copies.append(copy)

    x_all = jnp.concatenate([x[...] for x in x_refs], axis=0)
    for j in range(2):
        part = dot(x_all, w_ref[:, j * 256 : (j + 1) * 256]).astype(BF16).astype(F32)
        for i in range(count):
            seq_scr[i, 8 : 8 + LEN, j * 256 : (j + 1) * 256] = part[i * LEN : (i + 1) * LEN]
    z_scr[...] = dot(x_all, w_ref[:, 512:768]).astype(BF16)
    gate_scr[...] = dot(x_all, wg_ref[...])

    rows = lax.broadcasted_iota(jnp.int32, (LEN, LEN), 0)
    cols = lax.broadcasted_iota(jnp.int32, (LEN, LEN), 1)
    causal = rows >= cols
    strict = rows > cols
    ones_low = jnp.where(causal, 1.0, 0.0).astype(F32)
    levels = []
    for level in range(7):
        levels.append(
            ((rows >> (level + 1)) == (cols >> (level + 1)))
            & (((rows >> level) & 1) == 1)
            & (((cols >> level) & 1) == 0)
        )
    bias = gvec_ref[0:1, :]
    scale = gvec_ref[1:2, :]
    gain = gvec_ref[2:3, :]

    chains = []
    per = []
    for i in range(count):
        in_copies[i].wait()
        conv_rows = start_scr[i, 256:272, :].astype(F32)
        for j in range(3):
            for c in range(4):
                seq_scr[i, 5 + j : 6 + j, c * 128 : (c + 1) * 128] = conv_rows[
                    j * 4 + c : j * 4 + c + 1, :
                ]
        acts = []
        for c in range(4):
            lanes = slice(c * 128, (c + 1) * 128)
            conv = convw_ref[0:1, lanes] * seq_scr[i, 5 : 5 + LEN, lanes]
            for j in range(1, 4):
                conv = conv + convw_ref[j : j + 1, lanes] * seq_scr[i, 5 + j : 5 + j + LEN, lanes]
            acts.append(conv * (1.0 / (1.0 + jnp.exp(-conv))))
        query, key = acts[0], acts[1]
        query = query * (
            lax.rsqrt(jnp.sum(query * query, axis=-1, keepdims=True) + 1e-6) * DK ** (-0.5)
        )
        key = key * lax.rsqrt(jnp.sum(key * key, axis=-1, keepdims=True) + 1e-6)
        query = query.astype(BF16)
        key = key.astype(BF16)
        live = rows < lens[i]
        gates = gate_scr[i * LEN : (i + 1) * LEN, :]
        beta = jnp.where(live, 1.0 / (1.0 + jnp.exp(-gates)), 0.0)
        shifted = gates + bias
        softplus = jnp.maximum(shifted, 0.0) + jnp.log1p(jnp.exp(-jnp.abs(shifted)))
        decay = jnp.where(live, scale * softplus, 0.0)
        cum = jnp.dot(ones_low, decay, preferred_element_type=F32, precision=lax.Precision.HIGHEST)
        cum_t = cum.T
        key_t = key.T
        both = jnp.concatenate([key, query], axis=0)
        inner = dot(both, key_t)
        carry = jnp.concatenate(
            [start_scr[i, 0:128, :], start_scr[i, 128:256, :]], axis=1
        )
        reads = dot(both, carry)
        per.append((key_t, cum, carry))
        for j in range(2):
            cum_col = cum[:, 2 + j : 3 + j]
            cum_row = cum_t[2 + j : 3 + j, :]
            beta_col = beta[:, j : j + 1]
            weight = jnp.exp(jnp.where(causal, cum_col - cum_row, -1e30))
            lower = jnp.where(strict, beta_col * weight * inner[:LEN], 0.0).astype(BF16)
            mixing = (weight * inner[LEN:]).astype(BF16)
            grow = jnp.exp(cum_col)
            target = beta_col * (
                acts[2 + j] - grow * reads[:LEN, j * 128 : (j + 1) * 128]
            )
            chains.append(
                dict(
                    lower=lower,
                    mixing=mixing,
                    target=target.astype(BF16),
                    carried=grow * reads[LEN:, j * 128 : (j + 1) * 128],
                    last=jnp.exp(cum[LEN - 1 :, 2 + j : 3 + j] - cum_col),
                    inverse=jnp.where(rows == cols, 1.0, 0.0)
                    - jnp.where(levels[0], lower.astype(F32), 0.0),
                )
            )
    zero = jnp.zeros((), BF16)
    for level in range(1, 7):
        for ch in chains:
            inv = ch["inverse"].astype(BF16)
            step = dot(jnp.where(levels[level], ch["lower"], zero), inv)
            ch["inv"] = inv
            ch["step"] = step.astype(BF16)
        for ch in chains:
            ch["inverse"] = ch["inverse"] - dot(ch["inv"], ch["step"])
    for ch in chains:
        ch["update"] = dot(ch["inverse"].astype(BF16), ch["target"])
    out_copies = []
    for i in range(count):
        key_t, cum, carry = per[i]
        pair = chains[2 * i : 2 * i + 2]
        live = rows < lens[i]
        fresh = dot(
            key_t,
            jnp.concatenate([(ch["last"] * ch["update"]).astype(BF16) for ch in pair], axis=1),
        )
        for j, ch in enumerate(pair):
            lanes = slice(j * 128, (j + 1) * 128)
            keep = jnp.exp(cum[LEN - 1 :, 2 + j : 3 + j])
            state_scr[i, j] = keep * carry[:, lanes].astype(F32) + fresh[:, lanes]
        copy = pltpu.make_async_copy(state_scr.at[i], state_ref.at[rollouts[i]], out_sem.at[i])
        copy.start()
        out_copies.append(copy)
        for k in range(3):
            tail_scr[i, k : k + 1, :] = seq_scr[i, pl.ds(5 + k + lens[i], 1), :]
        copy = pltpu.make_async_copy(tail_scr.at[i], tail_ref.at[rollouts[i]], tail_sem.at[i])
        copy.start()
        out_copies.append(copy)
        for j, ch in enumerate(pair):
            lanes = slice(j * 128, (j + 1) * 128)
            read = ch["carried"] + dot(ch["mixing"], ch["update"].astype(BF16))
            inv_rms = lax.rsqrt(jnp.mean(read * read, axis=-1, keepdims=True) + 1e-6)
            z = z_scr[i * LEN : (i + 1) * LEN, lanes].astype(F32)
            silu = z * (1.0 / (1.0 + jnp.exp(-z)))
            core = jnp.where(live, read * inv_rms * gain * silu, 0.0)
            core_refs[i // 2][i % 2, :, lanes] = core.astype(BF16)
    for copy in out_copies:
        copy.wait()


def delta_call(pieces, first, shared, buffers):
    count = len(pieces)
    alias = buffers is not None
    out_shape = [jax.ShapeDtypeStruct((2, LEN, 2 * DV), BF16)] * (count // 2) + [
        jax.ShapeDtypeStruct((16, 2, DK, DV), F32),
        jax.ShapeDtypeStruct((16, 8, CONV), F32),
    ]
    base = len(shared) + count
    flops = count * (2 * LEN * 2048 * 896 + 2 * 2 * 15 * LEN**3 + 2 * 2 * 4 * LEN**3)
    out = pl.pallas_call(
        functools.partial(delta_kernel, count, first, alias),
        out_shape=out_shape,
        in_specs=[SMEM] * 3 + [VMEM] * 4 + [ANY] + [VMEM] * count + [ANY] * (2 if alias else 0),
        out_specs=[VMEM] * (count // 2) + [ANY] * 2,
        scratch_shapes=[
            pltpu.VMEM((count, SLOT_ROWS, 128), BF16),
            pltpu.VMEM((count, 144, CONV), F32),
            pltpu.VMEM((count * LEN, 2 * DV), BF16),
            pltpu.VMEM((count * LEN, 128), F32),
            pltpu.VMEM((count, 2, DK, DV), F32),
            pltpu.VMEM((count, 8, CONV), F32),
            pltpu.SemaphoreType.DMA((count,)),
            pltpu.SemaphoreType.DMA((count,)),
            pltpu.SemaphoreType.DMA((count,)),
        ],
        input_output_aliases={base: count // 2, base + 1: count // 2 + 1} if alias else {},
        compiler_params=pltpu.CompilerParams(vmem_limit_bytes=40 * 2**20),
        cost_estimate=pl.CostEstimate(
            flops=flops * 3, bytes_accessed=count * 2**20, transcendentals=0
        ),
    )(*shared, *pieces, *(buffers if alias else ()))
    return out[: count // 2], out[count // 2 :]


def project_kernel(zmap_ref, w_ref, *refs):
    core_refs = refs[:8]
    own_ref, other_ref, w_scr, acc_scr, sems = refs[8:]
    copies = []
    for d in range(8):
        copy = pltpu.make_async_copy(w_ref.at[:, zmap_ref[d]], w_scr.at[d], sems.at[d])
        copy.start()
        copies.append(copy)
    for d in range(8):
        copies[d].wait()
        lhs = core_refs[d][...].reshape(2 * LEN, 2 * DV)
        for n in range(4):
            lanes = slice(n * 512, (n + 1) * 512)
            part = dot(lhs, w_scr[d, :, :, lanes].reshape(2 * DV, 512))
            if d == 0:
                acc_scr[:, lanes] = part
            else:
                acc_scr[:, lanes] += part
    own_ref[...] = acc_scr[:LEN]
    other_ref[...] = acc_scr[LEN:].astype(BF16)


def project_call(zmap, w_all, cores):
    return pl.pallas_call(
        project_kernel,
        out_shape=[
            jax.ShapeDtypeStruct((LEN, 2048), F32),
            jax.ShapeDtypeStruct((LEN, 2048), BF16),
        ],
        in_specs=[SMEM, ANY] + [VMEM] * 8,
        out_specs=[VMEM] * 2,
        scratch_shapes=[
            pltpu.VMEM((8, 16, 16, 2048), BF16),
            pltpu.VMEM((2 * LEN, 2048), F32),
            pltpu.SemaphoreType.DMA((8,)),
        ],
        compiler_params=pltpu.CompilerParams(vmem_limit_bytes=40 * 2**20),
        cost_estimate=pl.CostEstimate(
            flops=2 * 256 * 2048 * 2048, bytes_accessed=11 * 2**20, transcendentals=0
        ),
    )(zmap, w_all, *cores)


def ring(shift):
    return [(2 * z + c, 2 * ((z + shift) % 8) + c) for z in range(8) for c in range(2)]


SWAP = [(i, i ^ 1) for i in range(16)]
SAME_CORE = [[2 * z + c for z in range(8)] for c in range(2)]


def move(values, shift):
    return lax.ppermute(values, "sp", ring(shift))


def swap(values):
    return lax.ppermute(values, "sp", SWAP)


def per_device(
    hidden,
    lengths,
    source_slot,
    old_state,
    old_conv,
    w_in,
    w_gates,
    conv_weight,
    decay_scale,
    dt_bias,
    norm_gain,
    w_out,
):
    owner = lax.axis_index("dp")
    place = lax.axis_index("sp")
    level, core = place // 2, place % 2
    order = [0]
    for d in (1, 2, 3):
        order += [-d, d]
    order += [4]
    zs = jnp.stack([(level + o) % 8 for o in order]).astype(jnp.int32)
    both = jnp.stack([2 * zs + core, 2 * zs + 1 - core], axis=1).reshape(16)
    ids = jnp.concatenate([both, jnp.full((8,), owner, jnp.int32)]).astype(jnp.int32)

    conv_rows = jnp.pad(old_conv[:, 0].reshape(16, 12, 128), ((0, 0), (0, 4), (0, 0)))
    packed = pl.pallas_call(
        pack_kernel,
        out_shape=jax.ShapeDtypeStruct((SLOTS, SLOT_ROWS, 128), BF16),
        in_specs=[SMEM, SMEM, VMEM, VMEM],
        out_specs=VMEM,
        scratch_shapes=[pltpu.SMEM((40,), jnp.int32)],
        compiler_params=pltpu.CompilerParams(vmem_limit_bytes=24 * 2**20),
    )(ids[16:17], source_slot, old_state[:, 0], conv_rows)
    arrived = lax.all_to_all(packed, "dp", split_axis=0, concat_axis=0, tiled=True)

    slice_out = lax.dynamic_slice_in_dim(w_out[0], owner * 16, 16, 0)
    sent = jnp.broadcast_to(slice_out[None], (8, 16, 2048))
    heads_out = lax.all_to_all(
        sent, "sp", split_axis=0, concat_axis=0, tiled=True, axis_index_groups=SAME_CORE
    )
    w_all = lax.all_gather(heads_out, "dp", axis=0, tiled=False)

    own = hidden[0]
    pieces = [own, swap(own)]
    ahead = behind = own
    for _ in range(3):
        ahead, behind = move(ahead, 1), move(behind, -1)
        pieces += [ahead, swap(ahead), behind, swap(behind)]
    upper = move(ahead[:64], 1)
    lower = move(behind[64:], -1)
    far = jnp.concatenate([upper, lower], axis=0)
    pieces += [far, swap(far)]

    gates = jnp.pad(w_gates[:, 0], ((0, 0), (0, 124)))
    lanes = jnp.zeros((8, 128), F32)
    lanes = lanes.at[0, 2:4].set(dt_bias[0]).at[1, 2:4].set(-decay_scale[0]).at[2].set(norm_gain)
    shared = (ids, source_slot, lengths, w_in[:, 0], gates, conv_weight[0], lanes, arrived)

    cores = {}
    buffers = None
    for group in ((1, 2), (3, 4), (5, 6), (7,), (0,)):
        members = [p for g in group for p in pieces[2 * g : 2 * g + 2]]
        done, buffers = delta_call(members, 2 * group[0], shared, buffers)
        for g, part in zip(group, done):
            cores[g] = move(part, order[g]) if g else part
    new_state, tails = buffers

    opposite = [0, 2, 1, 4, 3, 6, 5, 7]
    arrived_cores = [cores[opposite[g]] for g in range(8)]
    mine, theirs = project_call(zs, w_all, arrived_cores)
    layer_out = (mine + swap(theirs).astype(F32)).astype(BF16)
    new_conv = tails[:, :3].astype(BF16)
    return layer_out[None], new_state[:, None], new_conv[:, None]


def solution(mesh):
    in_specs = (
        P(("dp", "sp"), None, None),
        P("dp"),
        P(),
        P("dp", "sp", None, None, None),
        P("dp", "sp", None, None),
        P(None, "sp", None),
        P(None, "sp", None),
        P("sp", None, None),
        P("sp", None),
        P("sp", None),
        P(),
        P("sp", None, None),
    )
    out_specs = (
        P(("dp", "sp"), None, None),
        P("dp", "sp", None, None, None),
        P("dp", "sp", None, None),
    )
    return jax.shard_map(
        per_device, mesh=mesh, in_specs=in_specs, out_specs=out_specs, check_vma=False
    )
```

```python
import functools

import jax
import jax.numpy as jnp
from jax import lax
from jax.experimental import pallas as pl
from jax.experimental.pallas import tpu as pltpu
from jax.sharding import PartitionSpec as P

F32 = jnp.float32
BF16 = jnp.bfloat16
LEN = 128
DK = 128
DV = 128
CONV = 512
SLOTS = 32
SLOT_ROWS = 272
GROUP = 4
NLEVEL = 7
EARLY = True
SMEM = pl.BlockSpec(memory_space=pltpu.SMEM)
VMEM = pl.BlockSpec(memory_space=pltpu.VMEM)
ANY = pl.BlockSpec(memory_space=pltpu.HBM)


def dot(lhs, rhs):
    return jnp.dot(lhs, rhs, preferred_element_type=F32)


def pack_kernel(info_ref, source_ref, state_ref, conv_ref, out_ref, slot_ref, src_scr):
    me = info_ref[0]

    def one_target(target, _):
        found = jnp.int32(0)
        for i in range(16):
            value = source_ref[target * 16 + i]
            src_scr[target * 2 + found] = value & 15
            found = jnp.minimum(found + jnp.where((value >> 4) == me, 1, 0), 2)
        return 0

    lax.fori_loop(0, 16, one_target, 0)

    def one_slot(slot, _):
        src = src_scr[slot] & 15
        for j in range(2):
            out_ref[slot, j * 128 : (j + 1) * 128, :] = state_ref[src, j].astype(BF16)
        out_ref[slot, 256:272, :] = conv_ref[src]
        return 0

    lax.fori_loop(0, SLOTS, one_slot, 0)

    for i in range(16):
        src_scr[i] = 0

    def one_wanted(i, _):
        origin = (source_ref[me * 16 + i] >> 4) & 15
        rank = jnp.minimum(src_scr[origin], 1)
        src_scr[origin] = rank + 1
        slot_ref[i] = origin * 2 + rank
        return 0

    lax.fori_loop(0, 16, one_wanted, 0)


def sigmoid(values):
    return 1.0 / (1.0 + jnp.exp(-values))


def delta_kernel(
    slots_ref,
    lengths_ref,
    dtb_ref,
    scale_ref,
    x_ref,
    w_ref,
    wg_ref,
    convw_ref,
    gain_ref,
    *refs,
):
    start_refs = refs[:GROUP]
    core_ref, state_ref, tail_ref, seq_scr, z_scr = refs[GROUP:]
    group = pl.program_id(0)
    lens = [lengths_ref[group * GROUP + i] for i in range(GROUP)]

    x_all = x_ref[...].reshape(GROUP * LEN, 2048)
    gates_all = lax.dot_general(
        wg_ref[...], x_all, (((1,), (1,)), ((), ())), preferred_element_type=F32
    )[:8]
    for j in range(2):
        part = dot(x_all, w_ref[:, j * 256 : (j + 1) * 256]).astype(BF16).astype(F32)
        for i in range(GROUP):
            seq_scr[i, 8 : 8 + LEN, j * 256 : (j + 1) * 256] = part[i * LEN : (i + 1) * LEN]
    z_scr[...] = dot(x_all, w_ref[:, 512:768]).astype(BF16)

    rows = lax.broadcasted_iota(jnp.int32, (LEN, LEN), 0)
    cols = lax.broadcasted_iota(jnp.int32, (LEN, LEN), 1)
    causal = rows >= cols
    strict = rows > cols
    ones_up = jnp.where(rows <= cols, 1.0, 0.0).astype(F32)
    levels = []
    for level in range(7):
        levels.append(
            ((rows >> (level + 1)) == (cols >> (level + 1)))
            & (((rows >> level) & 1) == 1)
            & (((cols >> level) & 1) == 0)
        )
    gain = gain_ref[...]
    line = lax.broadcasted_iota(jnp.int32, (8, LEN), 0)
    token = lax.broadcasted_iota(jnp.int32, (8, LEN), 1)
    bias = jnp.where(line == 2, dtb_ref[0, 0], dtb_ref[0, 1])
    scale = jnp.where(line == 2, -scale_ref[0, 0], -scale_ref[0, 1])

    chains = []
    per = []
    for i in range(GROUP):
        conv_rows = start_refs[i][0, 256:272, :].astype(F32)
        for j in range(3):
            for c in range(4):
                seq_scr[i, 5 + j : 6 + j, c * 128 : (c + 1) * 128] = conv_rows[
                    j * 4 + c : j * 4 + c + 1, :
                ]
        acts = []
        for c in range(4):
            lanes = slice(c * 128, (c + 1) * 128)
            conv = convw_ref[0:1, lanes] * seq_scr[i, 5 : 5 + LEN, lanes]
            for j in range(1, 4):
                conv = conv + convw_ref[j : j + 1, lanes] * seq_scr[i, 5 + j : 5 + j + LEN, lanes]
            acts.append(conv * sigmoid(conv))
        query, key = acts[0], acts[1]
        query = query * (
            lax.rsqrt(jnp.sum(query * query, axis=-1, keepdims=True) + 1e-6) * DK ** (-0.5)
        )
        key = key * lax.rsqrt(jnp.sum(key * key, axis=-1, keepdims=True) + 1e-6)
        query = query.astype(BF16)
        key = key.astype(BF16)
        gates = gates_all[:, i * LEN : (i + 1) * LEN]
        alive = token < lens[i]
        beta = jnp.where(alive, sigmoid(gates), 0.0)
        shifted = gates + bias
        softplus = jnp.maximum(shifted, 0.0) + jnp.log1p(jnp.exp(-jnp.abs(shifted)))
        decay = jnp.where(alive, scale * softplus, 0.0)
        cum = jnp.dot(decay, ones_up, preferred_element_type=F32, precision=lax.Precision.HIGHEST)
        columns = jnp.where(line < 2, beta, cum).T
        key_t = key.T
        both = jnp.concatenate([key, query], axis=0)
        inner = dot(both, key_t)
        carry = jnp.concatenate([start_refs[i][0, 0:128, :], start_refs[i][0, 128:256, :]], axis=1)
        reads = dot(both, carry)
        per.append((key_t, cum, carry))
        for j in range(2):
            cum_col = columns[:, 2 + j : 3 + j]
            cum_row = cum[2 + j : 3 + j, :]
            beta_col = columns[:, j : j + 1]
            weight = jnp.exp(jnp.where(causal, cum_col - cum_row, -1e30))
            lower = jnp.where(strict, beta_col * weight * inner[:LEN], 0.0).astype(BF16)
            mixing = (weight * inner[LEN:]).astype(BF16)
            grow = jnp.exp(cum_col)
            target = beta_col * (acts[2 + j] - grow * reads[:LEN, j * 128 : (j + 1) * 128])
            chains.append(
                dict(
                    lower=lower,
                    mixing=mixing,
                    target=target.astype(BF16),
                    carried=grow * reads[LEN:, j * 128 : (j + 1) * 128],
                    last=jnp.exp(cum_row[:, LEN - 1 :] - cum_col),
                    inverse=jnp.where(rows == cols, 1.0, 0.0)
                    - jnp.where(levels[0], lower.astype(F32), 0.0),
                )
            )
    zero = jnp.zeros((), BF16)
    for level in range(1, NLEVEL):
        for ch in chains:
            inv = ch["inverse"].astype(BF16)
            step = dot(jnp.where(levels[level], ch["lower"], zero), inv)
            ch["inv"] = inv
            ch["step"] = step.astype(BF16)
        for ch in chains:
            ch["inverse"] = ch["inverse"] - dot(ch["inv"], ch["step"])
    for ch in chains:
        ch["update"] = dot(ch["inverse"].astype(BF16), ch["target"])
    for i in range(GROUP):
        key_t, cum, carry = per[i]
        pair = chains[2 * i : 2 * i + 2]
        live = rows < lens[i]
        fresh = dot(
            key_t,
            jnp.concatenate([(ch["last"] * ch["update"]).astype(BF16) for ch in pair], axis=1),
        )
        for j, ch in enumerate(pair):
            lanes = slice(j * 128, (j + 1) * 128)
            keep = jnp.exp(cum[2 + j : 3 + j, LEN - 1 :])
            state_ref[i, j] = keep * carry[:, lanes].astype(F32) + fresh[:, lanes]
        for k in range(3):
            tail_ref[i, k : k + 1, :] = seq_scr[i, pl.ds(5 + k + lens[i], 1), :]
        tail_ref[i, 3:8, :] = jnp.zeros((5, CONV), F32)
        for j, ch in enumerate(pair):
            lanes = slice(j * 128, (j + 1) * 128)
            read = ch["carried"] + dot(ch["mixing"], ch["update"].astype(BF16))
            inv_rms = lax.rsqrt(jnp.mean(read * read, axis=-1, keepdims=True) + 1e-6)
            z = z_scr[i * LEN : (i + 1) * LEN, lanes].astype(F32)
            core = jnp.where(live, read * inv_rms * gain * (z * sigmoid(z)), 0.0)
            core_ref[i, :, lanes] = core.astype(BF16)


def delta_call(slots, lengths, dt_bias, decay_scale, rows, w_in, gates, conv_weight, gain, arrived):
    whole = lambda *shape: pl.BlockSpec(shape, lambda s, *_: (0,) * len(shape))
    start = [
        pl.BlockSpec((1, SLOT_ROWS, 128), lambda s, slot, *_, i=i: (slot[s * GROUP + i], 0, 0))
        for i in range(GROUP)
    ]
    return pl.pallas_call(
        delta_kernel,
        out_shape=[
            jax.ShapeDtypeStruct((16, LEN, 2 * DV), BF16),
            jax.ShapeDtypeStruct((16, 2, DK, DV), F32),
            jax.ShapeDtypeStruct((16, 8, CONV), F32),
        ],
        grid_spec=pltpu.PrefetchScalarGridSpec(
            num_scalar_prefetch=4,
            grid=(16 // GROUP,),
            in_specs=[
                pl.BlockSpec((GROUP, LEN, 2048), lambda s, *_: (s, 0, 0)),
                whole(2048, 768),
                whole(16, 2048),
                whole(4, CONV),
                whole(1, DV),
            ]
            + start,
            out_specs=[
                pl.BlockSpec((GROUP, LEN, 2 * DV), lambda s, *_: (s, 0, 0)),
                pl.BlockSpec((GROUP, 2, DK, DV), lambda s, *_: (s, 0, 0, 0)),
                pl.BlockSpec((GROUP, 8, CONV), lambda s, *_: (s, 0, 0)),
            ],
            scratch_shapes=[
                pltpu.VMEM((GROUP, 144, CONV), F32),
                pltpu.VMEM((GROUP * LEN, 2 * DV), BF16),
            ],
        ),
        compiler_params=pltpu.CompilerParams(vmem_limit_bytes=56 * 2**20),
        cost_estimate=pl.CostEstimate(
            flops=20_000_000_000, bytes_accessed=20 * 2**20, transcendentals=0
        ),
    )(slots, lengths, dt_bias, decay_scale, rows, w_in, gates, conv_weight, gain, *[arrived] * GROUP)


def project_kernel(first, parts, info_ref, xmap_ref, *refs):
    w_refs = refs[:parts]
    core_ref = refs[parts]
    own_ref, other_ref, w_scr, row_scr, own_scr, other_scr, sems, out_sems = refs[-8:]
    level, core = info_ref[1], info_ref[2]
    blocks = [(ref, j) for ref in w_refs for j in range(ref.shape[0])]
    copies = []
    for i, (ref, j) in enumerate(blocks):
        copy = pltpu.make_async_copy(
            ref.at[j], w_scr.at[i // 2, :, :, pl.ds(i % 2 * 128, 128)], sems.at[i]
        )
        copy.start()
        copies.append(copy)
    for i in range(8):
        chip = level ^ (4 * (i & 1) + (i & 2) + (i >> 2))
        lanes = slice(i * 256, (i + 1) * 256)
        row_scr[0:LEN, lanes] = core_ref[2 * chip + core]
        row_scr[LEN:, lanes] = core_ref[2 * chip + 1 - core]
    out = []
    for n in range(len(blocks) // 2):
        copies[2 * n].wait()
        copies[2 * n + 1].wait()
        acc = dot(row_scr[...], w_scr[n].reshape(8 * 256, 256))
        for k in range(2):
            spot = pl.ds(pl.multiple_of(xmap_ref[first + 2 * n + k] * 128, 128), 128)
            own_scr[2 * n + k] = acc[:LEN, k * 128 : (k + 1) * 128]
            other_scr[2 * n + k] = acc[LEN:, k * 128 : (k + 1) * 128].astype(BF16)
            out.append(
                pltpu.make_async_copy(own_scr.at[2 * n + k], own_ref.at[:, spot], out_sems.at[0, 2 * n + k])
            )
            out.append(
                pltpu.make_async_copy(
                    other_scr.at[2 * n + k], other_ref.at[:, spot], out_sems.at[1, 2 * n + k]
                )
            )
            out[-2].start()
            out[-1].start()
    for copy in out:
        copy.wait()


def project_call(info, xmap, weights, first, cores, most):
    parts = len(weights)
    blocks = sum(w.shape[0] for w in weights)
    return pl.pallas_call(
        functools.partial(project_kernel, first, parts),
        out_shape=[
            jax.ShapeDtypeStruct((LEN, 2048), F32),
            jax.ShapeDtypeStruct((LEN, 2048), BF16),
        ],
        in_specs=[SMEM] * 2 + [ANY] * parts + [VMEM] + [ANY] * (2 if most else 0),
        out_specs=[ANY] * 2,
        scratch_shapes=[
            pltpu.VMEM((blocks // 2, 8, 256, 256), BF16),
            pltpu.VMEM((2 * LEN, 8 * 256), BF16),
            pltpu.VMEM((blocks, LEN, 128), F32),
            pltpu.VMEM((blocks, LEN, 128), BF16),
            pltpu.SemaphoreType.DMA((blocks,)),
            pltpu.SemaphoreType.DMA((2, blocks)),
        ],
        input_output_aliases={3 + parts: 0, 4 + parts: 1} if most else {},
        compiler_params=pltpu.CompilerParams(vmem_limit_bytes=58 * 2**20),
        cost_estimate=pl.CostEstimate(
            flops=2 * 256 * 2048 * 128 * blocks, bytes_accessed=blocks * 2**19, transcendentals=0
        ),
    )(info, xmap, *weights, cores, *(most or ()))


def across(shift, first):
    pairs = []
    for x in range(4):
        for y in range(4):
            for s in range(16):
                if (s % 2 == 0) != first:
                    to = x * 4 + (y + shift) % 4
                else:
                    to = ((x + shift) % 4) * 4 + y
                pairs.append(((x * 4 + y) * 16 + s, to * 16 + s))
    return pairs


SWAP = [(i, i ^ 1) for i in range(16)]
LINES = [[(4 * q + a) * 16 + 2 * z for q in range(4)] for a in range(4) for z in range(8)]
LINES += [[(4 * a + q) * 16 + 2 * z + 1 for q in range(4)] for a in range(4) for z in range(8)]
SAME_CORE = [[2 * z + c for z in range(8)] for c in range(2)]


def apart(bit):
    return [(2 * z + c, 2 * (z ^ bit) + c) for z in range(8) for c in range(2)]


def swap(values):
    return lax.ppermute(values, "sp", SWAP)


def cross(values, shift, first):
    return lax.ppermute(values, ("dp", "sp"), across(shift, first))


def after(value, *others):
    return lax.optimization_barrier((value, *others))[0]


def per_device(
    hidden,
    lengths,
    source_slot,
    old_state,
    old_conv,
    w_in,
    w_gates,
    conv_weight,
    decay_scale,
    dt_bias,
    norm_gain,
    w_out,
):
    owner = lax.axis_index("dp")
    place = lax.axis_index("sp")
    level, core = place // 2, place % 2
    info = jnp.stack([owner, level, core, owner]).astype(jnp.int32)
    px, py = owner // 4, owner % 4
    xmap = []
    for q in range(4):
        for o in (0, -1, 1, 2):
            near = (py + o) % 4 + 4 * q
            turned = 4 * ((px + o) % 4) + q
            xmap.append(jnp.where(core == 0, near, turned))
    xmap = jnp.stack(xmap).astype(jnp.int32)

    gathered = lax.all_gather(hidden[0], "sp", axis=0, tiled=False)

    conv_rows = jnp.pad(old_conv[:, 0].reshape(16, 12, 128), ((0, 0), (0, 4), (0, 0)))
    packed, slots = pl.pallas_call(
        pack_kernel,
        out_shape=[
            jax.ShapeDtypeStruct((SLOTS, SLOT_ROWS, 128), BF16),
            jax.ShapeDtypeStruct((16,), jnp.int32),
        ],
        in_specs=[SMEM, SMEM, VMEM, VMEM],
        out_specs=[VMEM, SMEM],
        scratch_shapes=[pltpu.SMEM((40,), jnp.int32)],
        compiler_params=pltpu.CompilerParams(vmem_limit_bytes=24 * 2**20),
    )(info, source_slot, old_state[:, 0], conv_rows)
    arrived = lax.all_to_all(packed, "dp", split_axis=0, concat_axis=0, tiled=True)

    share = lax.dynamic_slice_in_dim(w_out[0], owner * 128, 128, 1)[None]
    share = jnp.concatenate([share, lax.ppermute(share, "sp", apart(4))], axis=0)
    share = after(share, packed)
    share = jnp.concatenate([share, lax.ppermute(share, "sp", apart(2))], axis=0)
    share = after(share, arrived) if EARLY else share
    share = jnp.concatenate([share, lax.ppermute(share, "sp", apart(1))], axis=0)
    f1, g1 = cross(share, 1, False), cross(share, -1, False)
    f2, g2 = cross(f1[:4], 1, False), cross(g1[4:], -1, False)
    line = jnp.stack([share, f1, g1, jnp.concatenate([f2, g2], axis=0)])
    weights = lax.all_gather(
        line, ("dp", "sp"), axis=0, tiled=True, axis_index_groups=LINES
    )

    gates = jnp.pad(w_gates[:, 0].T, ((0, 12), (0, 0)))
    cores, new_state, tails = delta_call(
        slots,
        lengths,
        dt_bias,
        decay_scale,
        after(gathered, line),
        w_in[:, 0],
        gates,
        conv_weight[0],
        norm_gain[None],
        arrived,
    )
    cores = lax.all_to_all(
        cores, "sp", split_axis=0, concat_axis=0, tiled=True, axis_index_groups=SAME_CORE
    )
    mine, theirs = project_call(info, xmap, (weights,), 0, cores, None)
    layer_out = (mine + swap(theirs).astype(F32)).astype(BF16)
    new_conv = tails[:, :3].astype(BF16)
    return layer_out[None], new_state[:, None], new_conv[:, None]


def solution(mesh):
    in_specs = (
        P(("dp", "sp"), None, None),
        P("dp"),
        P(),
        P("dp", "sp", None, None, None),
        P("dp", "sp", None, None),
        P(None, "sp", None),
        P(None, "sp", None),
        P("sp", None, None),
        P("sp", None),
        P("sp", None),
        P(),
        P("sp", None, None),
    )
    out_specs = (
        P(("dp", "sp"), None, None),
        P("dp", "sp", None, None, None),
        P("dp", "sp", None, None),
    )
    return jax.shard_map(
        per_device, mesh=mesh, in_specs=in_specs, out_specs=out_specs, check_vma=False
    )
```

```python
import functools

import jax
import jax.numpy as jnp
from jax import lax
from jax.experimental import pallas as pl
from jax.experimental.pallas import tpu as pltpu
from jax.sharding import PartitionSpec as P

F32 = jnp.float32
BF16 = jnp.bfloat16
LEN = 128
DK = 128
DV = 128
CONV = 512
SLOTS = 32
SLOT_ROWS = 272
GROUP = 4
NLEVEL = 7
ORDER = (7, 5, 6, 3, 4, 1, 2, 0)
SMEM = pl.BlockSpec(memory_space=pltpu.SMEM)
VMEM = pl.BlockSpec(memory_space=pltpu.VMEM)
ANY = pl.BlockSpec(memory_space=pltpu.HBM)


def dot(lhs, rhs):
    return jnp.dot(lhs, rhs, preferred_element_type=F32)


def pack_kernel(info_ref, source_ref, state_ref, conv_ref, out_ref, slot_ref, src_scr):
    me = info_ref[0]

    def one_target(target, _):
        found = jnp.int32(0)
        for i in range(16):
            value = source_ref[target * 16 + i]
            src_scr[target * 2 + found] = value & 15
            found = jnp.minimum(found + jnp.where((value >> 4) == me, 1, 0), 2)
        return 0

    lax.fori_loop(0, 16, one_target, 0)

    def one_slot(slot, _):
        src = src_scr[slot] & 15
        for j in range(2):
            out_ref[slot, j * 128 : (j + 1) * 128, :] = state_ref[src, j].astype(BF16)
        out_ref[slot, 256:272, :] = conv_ref[src]
        return 0

    lax.fori_loop(0, SLOTS, one_slot, 0)

    for i in range(16):
        src_scr[i] = 0

    def one_wanted(i, _):
        origin = (source_ref[me * 16 + i] >> 4) & 15
        rank = jnp.minimum(src_scr[origin], 1)
        src_scr[origin] = rank + 1
        slot_ref[i] = origin * 2 + rank
        return 0

    lax.fori_loop(0, 16, one_wanted, 0)


def sigmoid(values):
    return 1.0 / (1.0 + jnp.exp(-values))


def delta_kernel(
    plan,
    first,
    unread,
    slots_ref,
    ids_ref,
    lengths_ref,
    dtb_ref,
    scale_ref,
    w_ref,
    wg_ref,
    convw_ref,
    gain_ref,
    *refs,
):
    start_refs = refs[:GROUP]
    x_refs = refs[GROUP : GROUP + len(plan)]
    refs = refs[GROUP + len(plan) + unread :]
    core_ref, state_ref, tail_ref, seq_scr, z_scr, x_scr, state_scr, tail_scr = refs[:8]
    x_sem, state_sem, tail_sem = refs[8:]
    group = pl.program_id(0)
    rollouts = [ids_ref[first + group * GROUP + i] for i in range(GROUP)]
    lens = [lengths_ref[r] for r in rollouts]

    def x_copy(k):
        at, size = plan[k]
        rows = pl.ds(at * LEN, size * LEN)
        return pltpu.make_async_copy(x_refs[k], x_scr.at[rows], x_sem.at[k])

    @pl.when(group == 0)
    def _():
        for k in range(len(plan)):
            x_copy(k).start()

    steps = x_scr.shape[0] // LEN // GROUP
    for step in range(steps):

        @pl.when(group == step)
        def _():
            for k in range(len(plan)):
                if plan[k][0] // GROUP == step:
                    x_copy(k).wait()

    x_all = x_scr[pl.ds(group * GROUP * LEN, GROUP * LEN), :]
    gates_all = lax.dot_general(
        wg_ref[...], x_all, (((1,), (1,)), ((), ())), preferred_element_type=F32
    )[:8]
    for j in range(2):
        part = dot(x_all, w_ref[:, j * 256 : (j + 1) * 256]).astype(BF16).astype(F32)
        for i in range(GROUP):
            seq_scr[i, 8 : 8 + LEN, j * 256 : (j + 1) * 256] = part[i * LEN : (i + 1) * LEN]
    z_scr[...] = dot(x_all, w_ref[:, 512:768]).astype(BF16)

    rows = lax.broadcasted_iota(jnp.int32, (LEN, LEN), 0)
    cols = lax.broadcasted_iota(jnp.int32, (LEN, LEN), 1)
    causal = rows >= cols
    strict = rows > cols
    ones_up = jnp.where(rows <= cols, 1.0, 0.0).astype(F32)
    levels = []
    for level in range(7):
        levels.append(
            ((rows >> (level + 1)) == (cols >> (level + 1)))
            & (((rows >> level) & 1) == 1)
            & (((cols >> level) & 1) == 0)
        )
    gain = gain_ref[...]
    line = lax.broadcasted_iota(jnp.int32, (8, LEN), 0)
    token = lax.broadcasted_iota(jnp.int32, (8, LEN), 1)
    bias = jnp.where(line == 2, dtb_ref[0, 0], dtb_ref[0, 1])
    scale = jnp.where(line == 2, -scale_ref[0, 0], -scale_ref[0, 1])

    chains = []
    per = []
    for i in range(GROUP):
        conv_rows = start_refs[i][0, 256:272, :].astype(F32)
        for j in range(3):
            for c in range(4):
                seq_scr[i, 5 + j : 6 + j, c * 128 : (c + 1) * 128] = conv_rows[
                    j * 4 + c : j * 4 + c + 1, :
                ]
        acts = []
        for c in range(4):
            lanes = slice(c * 128, (c + 1) * 128)
            conv = convw_ref[0:1, lanes] * seq_scr[i, 5 : 5 + LEN, lanes]
            for j in range(1, 4):
                conv = conv + convw_ref[j : j + 1, lanes] * seq_scr[i, 5 + j : 5 + j + LEN, lanes]
            acts.append(conv * sigmoid(conv))
        query, key = acts[0], acts[1]
        query = query * (
            lax.rsqrt(jnp.sum(query * query, axis=-1, keepdims=True) + 1e-6) * DK ** (-0.5)
        )
        key = key * lax.rsqrt(jnp.sum(key * key, axis=-1, keepdims=True) + 1e-6)
        query = query.astype(BF16)
        key = key.astype(BF16)
        gates = gates_all[:, i * LEN : (i + 1) * LEN]
        alive = token < lens[i]
        beta = jnp.where(alive, sigmoid(gates), 0.0)
        shifted = gates + bias
        softplus = jnp.maximum(shifted, 0.0) + jnp.log1p(jnp.exp(-jnp.abs(shifted)))
        decay = jnp.where(alive, scale * softplus, 0.0)
        cum = jnp.dot(decay, ones_up, preferred_element_type=F32, precision=lax.Precision.HIGHEST)
        columns = jnp.where(line < 2, beta, cum).T
        key_t = key.T
        both = jnp.concatenate([key, query], axis=0)
        inner = dot(both, key_t)
        carry = jnp.concatenate([start_refs[i][0, 0:128, :], start_refs[i][0, 128:256, :]], axis=1)
        reads = dot(both, carry)
        per.append((key_t, cum, carry))
        for j in range(2):
            cum_col = columns[:, 2 + j : 3 + j]
            cum_row = cum[2 + j : 3 + j, :]
            beta_col = columns[:, j : j + 1]
            weight = jnp.exp(jnp.where(causal, cum_col - cum_row, -1e30))
            lower = jnp.where(strict, beta_col * weight * inner[:LEN], 0.0).astype(BF16)
            mixing = (weight * inner[LEN:]).astype(BF16)
            grow = jnp.exp(cum_col)
            target = beta_col * (acts[2 + j] - grow * reads[:LEN, j * 128 : (j + 1) * 128])
            chains.append(
                dict(
                    lower=lower,
                    mixing=mixing,
                    target=target.astype(BF16),
                    carried=grow * reads[LEN:, j * 128 : (j + 1) * 128],
                    last=jnp.exp(cum_row[:, LEN - 1 :] - cum_col),
                    inverse=jnp.where(rows == cols, 1.0, 0.0)
                    - jnp.where(levels[0], lower.astype(F32), 0.0),
                )
            )
    zero = jnp.zeros((), BF16)
    for level in range(1, NLEVEL):
        for ch in chains:
            inv = ch["inverse"].astype(BF16)
            step = dot(jnp.where(levels[level], ch["lower"], zero), inv)
            ch["inv"] = inv
            ch["step"] = step.astype(BF16)
        for ch in chains:
            ch["inverse"] = ch["inverse"] - dot(ch["inv"], ch["step"])
    for ch in chains:
        ch["update"] = dot(ch["inverse"].astype(BF16), ch["target"])
    for i in range(GROUP):
        key_t, cum, carry = per[i]
        pair = chains[2 * i : 2 * i + 2]
        live = rows < lens[i]
        fresh = dot(
            key_t,
            jnp.concatenate([(ch["last"] * ch["update"]).astype(BF16) for ch in pair], axis=1),
        )
        for j, ch in enumerate(pair):
            lanes = slice(j * 128, (j + 1) * 128)
            keep = jnp.exp(cum[2 + j : 3 + j, LEN - 1 :])
            state_scr[group * GROUP + i, j] = keep * carry[:, lanes].astype(F32) + fresh[:, lanes]
        for k in range(3):
            tail_scr[group * GROUP + i, k : k + 1, :] = seq_scr[i, pl.ds(5 + k + lens[i], 1), :]
        tail_scr[group * GROUP + i, 3:8, :] = jnp.zeros((5, CONV), F32)
        pltpu.make_async_copy(
            state_scr.at[group * GROUP + i], state_ref.at[rollouts[i]], state_sem.at[group * GROUP + i]
        ).start()
        pltpu.make_async_copy(
            tail_scr.at[group * GROUP + i], tail_ref.at[rollouts[i]], tail_sem.at[group * GROUP + i]
        ).start()
        for j, ch in enumerate(pair):
            lanes = slice(j * 128, (j + 1) * 128)
            read = ch["carried"] + dot(ch["mixing"], ch["update"].astype(BF16))
            inv_rms = lax.rsqrt(jnp.mean(read * read, axis=-1, keepdims=True) + 1e-6)
            z = z_scr[i * LEN : (i + 1) * LEN, lanes].astype(F32)
            core = jnp.where(live, read * inv_rms * gain * (z * sigmoid(z)), 0.0)
            core_ref[i if i < 2 else 5 - i, :, lanes] = core.astype(BF16)

    @pl.when(group == steps - 1)
    def _():
        for k in range(steps * GROUP):
            r = ids_ref[first + k]
            pltpu.make_async_copy(state_scr.at[k], state_ref.at[r], state_sem.at[k]).wait()
            pltpu.make_async_copy(tail_scr.at[k], tail_ref.at[r], tail_sem.at[k]).wait()


def delta_call(scalars, arrays, arrived, pieces, plan, first, buffers, waits=()):
    count = sum(size for _, size in plan)
    whole = lambda *shape: pl.BlockSpec(shape, lambda s, *_: (0,) * len(shape))
    start = [
        pl.BlockSpec(
            (1, SLOT_ROWS, 128), lambda s, slot, ids, *_, i=i: (slot[ids[first + s * GROUP + i]], 0, 0)
        )
        for i in range(GROUP)
    ]
    extra = list(buffers or ()) + list(waits)
    base = len(scalars) + len(arrays) + GROUP + len(pieces)
    return pl.pallas_call(
        functools.partial(delta_kernel, plan, first, len(extra)),
        out_shape=[
            jax.ShapeDtypeStruct((count, LEN, 2 * DV), BF16),
            jax.ShapeDtypeStruct((16, 2, DK, DV), F32),
            jax.ShapeDtypeStruct((16, 8, CONV), F32),
        ],
        grid_spec=pltpu.PrefetchScalarGridSpec(
            num_scalar_prefetch=len(scalars),
            grid=(count // GROUP,),
            in_specs=[whole(2048, 768), whole(16, 2048), whole(4, CONV), whole(1, DV)]
            + start
            + [ANY] * (len(pieces) + len(extra)),
            out_specs=[pl.BlockSpec((GROUP, LEN, 2 * DV), lambda s, *_: (s, 0, 0)), ANY, ANY],
            scratch_shapes=[
                pltpu.VMEM((GROUP, 144, CONV), F32),
                pltpu.VMEM((GROUP * LEN, 2 * DV), BF16),
                pltpu.VMEM((count * LEN, 2048), BF16),
                pltpu.VMEM((count, 2, DK, DV), F32),
                pltpu.VMEM((count, 8, CONV), F32),
                pltpu.SemaphoreType.DMA((len(plan),)),
                pltpu.SemaphoreType.DMA((count,)),
                pltpu.SemaphoreType.DMA((count,)),
            ],
        ),
        input_output_aliases={base: 1, base + 1: 2} if buffers else {},
        compiler_params=pltpu.CompilerParams(vmem_limit_bytes=40 * 2**20),
        cost_estimate=pl.CostEstimate(
            flops=count * 1_250_000_000, bytes_accessed=count * 2**20, transcendentals=0
        ),
    )(*scalars, *arrays, *[arrived] * GROUP, *pieces, *extra)


def project_kernel(info_ref, w_ref, *refs):
    core_refs = refs[:8]
    own_ref, other_ref, w_scr, row_scr, sems = refs[8:]
    copies = []
    for q in range(4):
        some = pl.ds(4 * q, 4)
        copy = pltpu.make_async_copy(w_ref.at[some], w_scr.at[some], sems.at[q])
        copy.start()
        copies.append(copy)
    for d in range(8):
        spot = info_ref[4 + d]
        row_scr[spot, 0:LEN] = core_refs[d][1 if d == 0 else 0]
        row_scr[spot, LEN:] = core_refs[d][0 if d == 0 else 1]
    lhs = jnp.concatenate([row_scr[i] for i in range(8)], axis=1)
    for q in range(4):
        copies[q].wait()
        for n in range(2):
            at = 4 * q + 2 * n
            rhs = [w_scr[at + k].reshape(8 * 256, 128) for k in range(2)]
            acc = dot(lhs, jnp.concatenate(rhs, axis=1))
            lanes = slice(q * 512 + n * 256, q * 512 + (n + 1) * 256)
            own_ref[:, lanes] = acc[:LEN]
            other_ref[:, lanes] = acc[LEN:].astype(BF16)


def project_call(info, weights, cores):
    return pl.pallas_call(
        project_kernel,
        out_shape=[
            jax.ShapeDtypeStruct((LEN, 2048), F32),
            jax.ShapeDtypeStruct((LEN, 2048), BF16),
        ],
        in_specs=[SMEM, ANY] + [VMEM] * 8,
        out_specs=[VMEM] * 2,
        scratch_shapes=[
            pltpu.VMEM((16, 8, 256, 128), BF16),
            pltpu.VMEM((8, 2 * LEN, 256), BF16),
            pltpu.SemaphoreType.DMA((4,)),
        ],
        compiler_params=pltpu.CompilerParams(vmem_limit_bytes=58 * 2**20),
        cost_estimate=pl.CostEstimate(
            flops=2 * 256 * 2048 * 128 * 16, bytes_accessed=10 * 2**20, transcendentals=0
        ),
    )(info, weights, *cores)


SWAP = [(i, i ^ 1) for i in range(16)]


def along(shift):
    return [(2 * z + c, 2 * ((z + (shift if c == 0 else -shift)) % 8) + c) for z in range(8) for c in range(2)]


def move(values, shift):
    return lax.ppermute(values, "sp", along(shift))


def swap(values):
    return lax.ppermute(values, "sp", SWAP)


def after(value, *others):
    return lax.optimization_barrier((value, *others))[0]


def per_device(
    hidden,
    lengths,
    source_slot,
    old_state,
    old_conv,
    w_in,
    w_gates,
    conv_weight,
    decay_scale,
    dt_bias,
    norm_gain,
    w_out,
):
    owner = lax.axis_index("dp")
    place = lax.axis_index("sp")
    level, core = place // 2, place % 2
    way = 1 - 2 * core
    zs, ids = [level], []
    for step in (1, 2, 3):
        for sign in (-1, 1):
            zs.append((level + sign * step * way) % 8)
            ids += [2 * zs[-1] + core, 2 * zs[-1] + 1 - core][::-sign]
    zs.append((level + 4) % 8)
    for chip in (zs[-1], level):
        ids += [2 * chip + core, 2 * chip + 1 - core]
    info = jnp.stack([owner, level, core, owner] + zs).astype(jnp.int32)
    ids = jnp.stack(ids).astype(jnp.int32)

    own = hidden[0]
    s0 = swap(own)

    conv_rows = jnp.pad(old_conv[:, 0].reshape(16, 12, 128), ((0, 0), (0, 4), (0, 0)))
    packed, slots = pl.pallas_call(
        pack_kernel,
        out_shape=[
            jax.ShapeDtypeStruct((SLOTS, SLOT_ROWS, 128), BF16),
            jax.ShapeDtypeStruct((16,), jnp.int32),
        ],
        in_specs=[SMEM, SMEM, VMEM, VMEM],
        out_specs=[VMEM, SMEM],
        scratch_shapes=[pltpu.SMEM((40,), jnp.int32)],
        compiler_params=pltpu.CompilerParams(vmem_limit_bytes=24 * 2**20),
    )(info, source_slot, old_state[:, 0], conv_rows)
    arrived = lax.all_to_all(packed, "dp", split_axis=0, concat_axis=0, tiled=True)

    held0 = jnp.concatenate([own, after(s0, packed)], axis=0)
    ring1 = move(held0, 1)
    arrived = after(arrived, ring1)
    held1 = after(ring1, arrived)
    ring2, w1 = move(held1, 1), swap(held1)

    share = lax.dynamic_slice_in_dim(w_out[0], owner // 2 * 256, 256, 1)
    heads = after(lax.all_gather(share, "sp", axis=0, tiled=False), held1)
    heads = lax.dynamic_slice(
        heads.reshape(8, 2, 256, 256), (0, core, 0, owner % 2 * 128), (8, 1, 256, 128)
    )[:, 0]
    weights = lax.all_gather(heads, "dp", axis=0, tiled=False)

    gates = jnp.pad(w_gates[:, 0].T, ((0, 12), (0, 0)))
    scalars = (slots, ids, lengths, dt_bias, decay_scale)
    arrays = (w_in[:, 0], gates, conv_weight[0], norm_gain[None])
    cores = [None] * 8
    plan = ((0, 2), (2, 2))
    done, *buffers = delta_call(scalars, arrays, arrived, (held1, w1), plan, 0, None, (heads,))
    held2 = after(ring2, done)
    ring3, w2 = move(held2, 1), swap(held2)
    cores[2], cores[1] = move(done[0:2], -1), move(done[2:4], 1)
    done, *buffers = delta_call(scalars, arrays, arrived, (held2, w2), plan, 4, buffers)
    cores[4], cores[3] = move(done[0:2], -2), move(done[2:4], 2)
    held3 = after(ring3, done, cores[1], cores[2])
    ring4, w3 = move(held3[:LEN], 1), swap(held3)
    done, *buffers = delta_call(scalars, arrays, arrived, (held3, w3), plan, 8, buffers)
    cores[6], cores[5] = move(done[0:2], -3), move(done[2:4], 3)
    ring4 = after(ring4, done, cores[3], cores[4])
    last = (ring4, swap(ring4), held0)
    plan = ((0, 1), (1, 1), (2, 2))
    done, *buffers = delta_call(scalars, arrays, arrived, last, plan, 12, buffers)
    done = after(done, cores[5], cores[6])
    cores[7], cores[0] = move(done[0:2], 4), done[2:4]
    new_state, tails = buffers
    new_conv = tails[:, :3].astype(BF16)
    cores[0] = after(cores[0], new_conv)
    mine, theirs = project_call(info, weights, cores)
    layer_out = (mine + swap(theirs).astype(F32)).astype(BF16)
    return layer_out[None], new_state[:, None], new_conv[:, None]


def solution(mesh):
    in_specs = (
        P(("dp", "sp"), None, None),
        P("dp"),
        P(),
        P("dp", "sp", None, None, None),
        P("dp", "sp", None, None),
        P(None, "sp", None),
        P(None, "sp", None),
        P("sp", None, None),
        P("sp", None),
        P("sp", None),
        P(),
        P("sp", None, None),
    )
    out_specs = (
        P(("dp", "sp"), None, None),
        P("dp", "sp", None, None, None),
        P("dp", "sp", None, None),
    )
    return jax.shard_map(
        per_device, mesh=mesh, in_specs=in_specs, out_specs=out_specs, check_vma=False
    )
```

```python
import functools

import jax
import jax.numpy as jnp
from jax import lax
from jax.experimental import pallas as pl
from jax.experimental.pallas import tpu as pltpu
from jax.sharding import PartitionSpec as P

F32 = jnp.float32
BF16 = jnp.bfloat16
LEN = 128
DK = 128
DV = 128
CONV = 512
SLOTS = 32
SLOT_ROWS = 272
GROUP = 4
NLEVEL = 7
ORDER = (7, 5, 6, 3, 4, 1, 2, 0)
SMEM = pl.BlockSpec(memory_space=pltpu.SMEM)
VMEM = pl.BlockSpec(memory_space=pltpu.VMEM)
ANY = pl.BlockSpec(memory_space=pltpu.HBM)


def dot(lhs, rhs):
    return jnp.dot(lhs, rhs, preferred_element_type=F32)


def pack_kernel(info_ref, source_ref, state_ref, conv_ref, out_ref, slot_ref, src_scr):
    me = info_ref[0]

    def one_target(target, _):
        found = jnp.int32(0)
        for i in range(16):
            value = source_ref[target * 16 + i]
            src_scr[target * 2 + found] = value & 15
            found = jnp.minimum(found + jnp.where((value >> 4) == me, 1, 0), 2)
        return 0

    lax.fori_loop(0, 16, one_target, 0)

    def one_slot(slot, _):
        src = src_scr[slot] & 15
        for j in range(2):
            out_ref[slot, j * 128 : (j + 1) * 128, :] = state_ref[src, j].astype(BF16)
        out_ref[slot, 256:272, :] = conv_ref[src]
        return 0

    lax.fori_loop(0, SLOTS, one_slot, 0)

    for i in range(16):
        src_scr[i] = 0

    def one_wanted(i, _):
        origin = (source_ref[me * 16 + i] >> 4) & 15
        rank = jnp.minimum(src_scr[origin], 1)
        src_scr[origin] = rank + 1
        slot_ref[i] = origin * 2 + rank
        return 0

    lax.fori_loop(0, 16, one_wanted, 0)


def sigmoid(values):
    return 1.0 / (1.0 + jnp.exp(-values))


def delta_kernel(
    plan,
    first,
    unread,
    slots_ref,
    ids_ref,
    lengths_ref,
    dtb_ref,
    scale_ref,
    w_ref,
    wg_ref,
    convw_ref,
    gain_ref,
    *refs,
):
    size = min(GROUP, sum(n for _, n in plan))
    start_refs = refs[:size]
    x_refs = refs[size : size + len(plan)]
    refs = refs[size + len(plan) + unread :]
    core_ref, state_ref, tail_ref, seq_scr, z_scr, x_scr, state_scr, tail_scr = refs[:8]
    x_sem, state_sem, tail_sem = refs[8:]
    group = pl.program_id(0)
    rollouts = [ids_ref[first + group * size + i] for i in range(size)]
    lens = [lengths_ref[r] for r in rollouts]

    def x_copy(k):
        at, some = plan[k]
        rows = pl.ds(at * LEN, some * LEN)
        return pltpu.make_async_copy(x_refs[k], x_scr.at[rows], x_sem.at[k])

    @pl.when(group == 0)
    def _():
        for k in range(len(plan)):
            x_copy(k).start()

    steps = x_scr.shape[0] // LEN // size
    for step in range(steps):

        @pl.when(group == step)
        def _():
            for k in range(len(plan)):
                if plan[k][0] // size == step:
                    x_copy(k).wait()

    x_all = x_scr[pl.ds(group * size * LEN, size * LEN), :]
    gates_all = lax.dot_general(
        wg_ref[...], x_all, (((1,), (1,)), ((), ())), preferred_element_type=F32
    )[:8]
    for j in range(2):
        part = dot(x_all, w_ref[:, j * 256 : (j + 1) * 256]).astype(BF16).astype(F32)
        for i in range(size):
            seq_scr[i, 8 : 8 + LEN, j * 256 : (j + 1) * 256] = part[i * LEN : (i + 1) * LEN]
    z_scr[...] = dot(x_all, w_ref[:, 512:768]).astype(BF16)

    rows = lax.broadcasted_iota(jnp.int32, (LEN, LEN), 0)
    cols = lax.broadcasted_iota(jnp.int32, (LEN, LEN), 1)
    causal = rows >= cols
    strict = rows > cols
    ones_up = jnp.where(rows <= cols, 1.0, 0.0).astype(F32)
    levels = []
    for level in range(7):
        levels.append(
            ((rows >> (level + 1)) == (cols >> (level + 1)))
            & (((rows >> level) & 1) == 1)
            & (((cols >> level) & 1) == 0)
        )
    gain = gain_ref[...]
    line = lax.broadcasted_iota(jnp.int32, (8, LEN), 0)
    token = lax.broadcasted_iota(jnp.int32, (8, LEN), 1)
    bias = jnp.where(line == 2, dtb_ref[0, 0], dtb_ref[0, 1])
    scale = jnp.where(line == 2, -scale_ref[0, 0], -scale_ref[0, 1])

    chains = []
    per = []
    for i in range(size):
        conv_rows = start_refs[i][0, 256:272, :].astype(F32)
        for j in range(3):
            for c in range(4):
                seq_scr[i, 5 + j : 6 + j, c * 128 : (c + 1) * 128] = conv_rows[
                    j * 4 + c : j * 4 + c + 1, :
                ]
        acts = []
        for c in range(4):
            lanes = slice(c * 128, (c + 1) * 128)
            conv = convw_ref[0:1, lanes] * seq_scr[i, 5 : 5 + LEN, lanes]
            for j in range(1, 4):
                conv = conv + convw_ref[j : j + 1, lanes] * seq_scr[i, 5 + j : 5 + j + LEN, lanes]
            acts.append(conv * sigmoid(conv))
        query, key = acts[0], acts[1]
        query = query * (
            lax.rsqrt(jnp.sum(query * query, axis=-1, keepdims=True) + 1e-6) * DK ** (-0.5)
        )
        key = key * lax.rsqrt(jnp.sum(key * key, axis=-1, keepdims=True) + 1e-6)
        query = query.astype(BF16)
        key = key.astype(BF16)
        gates = gates_all[:, i * LEN : (i + 1) * LEN]
        alive = token < lens[i]
        beta = jnp.where(alive, sigmoid(gates), 0.0)
        shifted = gates + bias
        softplus = jnp.maximum(shifted, 0.0) + jnp.log1p(jnp.exp(-jnp.abs(shifted)))
        decay = jnp.where(alive, scale * softplus, 0.0)
        cum = jnp.dot(decay, ones_up, preferred_element_type=F32, precision=lax.Precision.HIGHEST)
        columns = jnp.where(line < 2, beta, cum).T
        key_t = key.T
        both = jnp.concatenate([key, query], axis=0)
        inner = dot(both, key_t)
        carry = jnp.concatenate([start_refs[i][0, 0:128, :], start_refs[i][0, 128:256, :]], axis=1)
        reads = dot(both, carry)
        per.append((key_t, cum, carry))
        for j in range(2):
            cum_col = columns[:, 2 + j : 3 + j]
            cum_row = cum[2 + j : 3 + j, :]
            beta_col = columns[:, j : j + 1]
            weight = jnp.exp(jnp.where(causal, cum_col - cum_row, -1e30))
            lower = jnp.where(strict, beta_col * weight * inner[:LEN], 0.0).astype(BF16)
            mixing = (weight * inner[LEN:]).astype(BF16)
            grow = jnp.exp(cum_col)
            target = beta_col * (acts[2 + j] - grow * reads[:LEN, j * 128 : (j + 1) * 128])
            chains.append(
                dict(
                    lower=lower,
                    mixing=mixing,
                    target=target.astype(BF16),
                    carried=grow * reads[LEN:, j * 128 : (j + 1) * 128],
                    last=jnp.exp(cum_row[:, LEN - 1 :] - cum_col),
                    inverse=jnp.where(rows == cols, 1.0, 0.0)
                    - jnp.where(levels[0], lower.astype(F32), 0.0),
                )
            )
    zero = jnp.zeros((), BF16)
    for level in range(1, NLEVEL):
        for ch in chains:
            inv = ch["inverse"].astype(BF16)
            step = dot(jnp.where(levels[level], ch["lower"], zero), inv)
            ch["inv"] = inv
            ch["step"] = step.astype(BF16)
        for ch in chains:
            ch["inverse"] = ch["inverse"] - dot(ch["inv"], ch["step"])
    for ch in chains:
        ch["update"] = dot(ch["inverse"].astype(BF16), ch["target"])
    for i in range(size):
        key_t, cum, carry = per[i]
        pair = chains[2 * i : 2 * i + 2]
        live = rows < lens[i]
        fresh = dot(
            key_t,
            jnp.concatenate([(ch["last"] * ch["update"]).astype(BF16) for ch in pair], axis=1),
        )
        for j, ch in enumerate(pair):
            lanes = slice(j * 128, (j + 1) * 128)
            keep = jnp.exp(cum[2 + j : 3 + j, LEN - 1 :])
            state_scr[group * size + i, j] = keep * carry[:, lanes].astype(F32) + fresh[:, lanes]
        for k in range(3):
            tail_scr[group * size + i, k : k + 1, :] = seq_scr[i, pl.ds(5 + k + lens[i], 1), :]
        tail_scr[group * size + i, 3:8, :] = jnp.zeros((5, CONV), F32)
        pltpu.make_async_copy(
            state_scr.at[group * size + i], state_ref.at[rollouts[i]], state_sem.at[group * size + i]
        ).start()
        pltpu.make_async_copy(
            tail_scr.at[group * size + i], tail_ref.at[rollouts[i]], tail_sem.at[group * size + i]
        ).start()
        for j, ch in enumerate(pair):
            lanes = slice(j * 128, (j + 1) * 128)
            read = ch["carried"] + dot(ch["mixing"], ch["update"].astype(BF16))
            inv_rms = lax.rsqrt(jnp.mean(read * read, axis=-1, keepdims=True) + 1e-6)
            z = z_scr[i * LEN : (i + 1) * LEN, lanes].astype(F32)
            core = jnp.where(live, read * inv_rms * gain * (z * sigmoid(z)), 0.0)
            core_ref[i if i < 2 else 5 - i, :, lanes] = core.astype(BF16)

    @pl.when(group == steps - 1)
    def _():
        for k in range(steps * size):
            r = ids_ref[first + k]
            pltpu.make_async_copy(state_scr.at[k], state_ref.at[r], state_sem.at[k]).wait()
            pltpu.make_async_copy(tail_scr.at[k], tail_ref.at[r], tail_sem.at[k]).wait()


def delta_call(scalars, arrays, arrived, pieces, plan, first, buffers, waits=()):
    count = sum(n for _, n in plan)
    size = min(GROUP, count)
    whole = lambda *shape: pl.BlockSpec(shape, lambda s, *_: (0,) * len(shape))
    start = [
        pl.BlockSpec(
            (1, SLOT_ROWS, 128), lambda s, slot, ids, *_, i=i: (slot[ids[first + s * size + i]], 0, 0)
        )
        for i in range(size)
    ]
    extra = list(buffers or ()) + list(waits)
    base = len(scalars) + len(arrays) + size + len(pieces)
    return pl.pallas_call(
        functools.partial(delta_kernel, plan, first, len(extra)),
        out_shape=[
            jax.ShapeDtypeStruct((count, LEN, 2 * DV), BF16),
            jax.ShapeDtypeStruct((16, 2, DK, DV), F32),
            jax.ShapeDtypeStruct((16, 8, CONV), F32),
        ],
        grid_spec=pltpu.PrefetchScalarGridSpec(
            num_scalar_prefetch=len(scalars),
            grid=(count // size,),
            in_specs=[whole(2048, 768), whole(16, 2048), whole(4, CONV), whole(1, DV)]
            + start
            + [ANY] * (len(pieces) + len(extra)),
            out_specs=[pl.BlockSpec((size, LEN, 2 * DV), lambda s, *_: (s, 0, 0)), ANY, ANY],
            scratch_shapes=[
                pltpu.VMEM((size, 144, CONV), F32),
                pltpu.VMEM((size * LEN, 2 * DV), BF16),
                pltpu.VMEM((count * LEN, 2048), BF16),
                pltpu.VMEM((count, 2, DK, DV), F32),
                pltpu.VMEM((count, 8, CONV), F32),
                pltpu.SemaphoreType.DMA((len(plan),)),
                pltpu.SemaphoreType.DMA((count,)),
                pltpu.SemaphoreType.DMA((count,)),
            ],
        ),
        input_output_aliases={base: 1, base + 1: 2} if buffers else {},
        compiler_params=pltpu.CompilerParams(vmem_limit_bytes=40 * 2**20),
        cost_estimate=pl.CostEstimate(
            flops=count * 1_250_000_000, bytes_accessed=count * 2**20, transcendentals=0
        ),
    )(*scalars, *arrays, *[arrived] * size, *pieces, *extra)


def project_kernel(info_ref, w_ref, *refs):
    core_refs = refs[:8]
    own_ref, other_ref, w_scr, row_scr, sems = refs[8:]
    copies = []
    for q in range(4):
        some = pl.ds(4 * q, 4)
        copy = pltpu.make_async_copy(w_ref.at[some], w_scr.at[some], sems.at[q])
        copy.start()
        copies.append(copy)
    for d in range(8):
        spot = info_ref[4 + d]
        row_scr[spot] = core_refs[d][...].reshape(2 * LEN, 2 * DV)
    lhs = jnp.concatenate([row_scr[i] for i in range(8)], axis=1)
    for q in range(4):
        copies[q].wait()
        for n in range(2):
            at = 4 * q + 2 * n
            rhs = [w_scr[at + k].reshape(8 * 256, 128) for k in range(2)]
            acc = dot(lhs, jnp.concatenate(rhs, axis=1))
            lanes = slice(q * 512 + n * 256, q * 512 + (n + 1) * 256)
            own_ref[:, lanes] = acc[:LEN]
            other_ref[:, lanes] = acc[LEN:].astype(BF16)


def project_call(info, weights, cores):
    return pl.pallas_call(
        project_kernel,
        out_shape=[
            jax.ShapeDtypeStruct((LEN, 2048), F32),
            jax.ShapeDtypeStruct((LEN, 2048), BF16),
        ],
        in_specs=[SMEM, ANY] + [VMEM] * 8,
        out_specs=[VMEM] * 2,
        scratch_shapes=[
            pltpu.VMEM((16, 8, 256, 128), BF16),
            pltpu.VMEM((8, 2 * LEN, 256), BF16),
            pltpu.SemaphoreType.DMA((4,)),
        ],
        compiler_params=pltpu.CompilerParams(vmem_limit_bytes=58 * 2**20),
        cost_estimate=pl.CostEstimate(
            flops=2 * 256 * 2048 * 128 * 16, bytes_accessed=10 * 2**20, transcendentals=0
        ),
    )(info, weights, *cores)


SWAP = [(i, i ^ 1) for i in range(16)]


def along(shift):
    return [(2 * z + c, 2 * ((z + (shift if c == 0 else -shift)) % 8) + c) for z in range(8) for c in range(2)]


def move(values, shift):
    return lax.ppermute(values, "sp", along(shift))


def swap(values):
    return lax.ppermute(values, "sp", SWAP)


def after(value, *others):
    return lax.optimization_barrier((value, *others))[0]


def per_device(
    hidden,
    lengths,
    source_slot,
    old_state,
    old_conv,
    w_in,
    w_gates,
    conv_weight,
    decay_scale,
    dt_bias,
    norm_gain,
    w_out,
):
    owner = lax.axis_index("dp")
    place = lax.axis_index("sp")
    level, core = place // 2, place % 2
    way = 1 - 2 * core
    zs, ids = [level], []
    for step in (1, 2, 3):
        for sign in (-1, 1):
            zs.append((level + sign * step * way) % 8)
            ids += [2 * zs[-1] + core, 2 * zs[-1] + 1 - core][::-sign]
    zs.append((level + 4) % 8)
    for chip in (zs[-1], level):
        ids += [2 * chip + core, 2 * chip + 1 - core]
    info = jnp.stack([owner, level, core, owner] + zs).astype(jnp.int32)
    ids = jnp.stack(ids).astype(jnp.int32)

    own = hidden[0]
    s0 = swap(own)

    conv_rows = jnp.pad(old_conv[:, 0].reshape(16, 12, 128), ((0, 0), (0, 4), (0, 0)))
    packed, slots = pl.pallas_call(
        pack_kernel,
        out_shape=[
            jax.ShapeDtypeStruct((SLOTS, SLOT_ROWS, 128), BF16),
            jax.ShapeDtypeStruct((16,), jnp.int32),
        ],
        in_specs=[SMEM, SMEM, VMEM, VMEM],
        out_specs=[VMEM, SMEM],
        scratch_shapes=[pltpu.SMEM((40,), jnp.int32)],
        compiler_params=pltpu.CompilerParams(vmem_limit_bytes=24 * 2**20),
    )(info, source_slot, old_state[:, 0], conv_rows)
    arrived = lax.all_to_all(packed, "dp", split_axis=0, concat_axis=0, tiled=True)

    held0 = jnp.concatenate([own, after(s0, packed)], axis=0)
    ring1 = move(held0, 1)
    arrived = after(arrived, ring1)
    held1 = after(ring1, arrived)
    ring2, w1 = move(held1, 1), swap(held1)

    share = lax.dynamic_slice_in_dim(w_out[0], owner // 2 * 256, 256, 1)
    spread = after(lax.all_gather(share, "sp", axis=0, tiled=False), held1)
    heads = lax.dynamic_slice(
        spread.reshape(8, 2, 256, 256), (0, core, 0, owner % 2 * 128), (8, 1, 256, 128)
    )[:, 0]
    weights = lax.all_gather(heads, "dp", axis=0, tiled=False)

    gates = jnp.pad(w_gates[:, 0].T, ((0, 12), (0, 0)))
    scalars = (slots, ids, lengths, dt_bias, decay_scale)
    arrays = (w_in[:, 0], gates, conv_weight[0], norm_gain[None])
    cores = [None] * 8
    plan = ((0, 2), (2, 2))
    done, *buffers = delta_call(scalars, arrays, arrived, (held1, w1), plan, 0, None, (spread,))
    held2 = after(ring2, done)
    ring3, w2 = move(held2, 1), swap(held2)
    cores[2], cores[1] = move(done[0:2], -1), move(done[2:4], 1)
    done, *buffers = delta_call(scalars, arrays, arrived, (held2, w2), plan, 4, buffers)
    cores[4], cores[3] = move(done[0:2], -2), move(done[2:4], 2)
    done, *buffers = delta_call(scalars, arrays, arrived, (held0,), ((0, 2),), 14, buffers)
    cores[0] = done
    held3 = after(ring3, done, cores[1], cores[2])
    ring4, w3 = move(held3[:LEN], 1), swap(held3)
    done, *buffers = delta_call(scalars, arrays, arrived, (held3, w3), plan, 8, buffers)
    cores[6], cores[5] = move(done[0:2], -3), move(done[2:4], 3)
    ring4 = after(ring4, done, cores[3], cores[4])
    plan = ((0, 1), (1, 1))
    done, *buffers = delta_call(scalars, arrays, arrived, (ring4, swap(ring4)), plan, 12, buffers)
    cores[7] = move(done, 4)
    new_state, tails = buffers
    new_conv = tails[:, :3].astype(BF16)
    cores[0], new_conv = lax.optimization_barrier((cores[0], new_conv))
    mine, theirs = project_call(info, weights, cores)
    layer_out = (mine + swap(theirs).astype(F32)).astype(BF16)
    return layer_out[None], new_state[:, None], new_conv[:, None]


def solution(mesh):
    in_specs = (
        P(("dp", "sp"), None, None),
        P("dp"),
        P(),
        P("dp", "sp", None, None, None),
        P("dp", "sp", None, None),
        P(None, "sp", None),
        P(None, "sp", None),
        P("sp", None, None),
        P("sp", None),
        P("sp", None),
        P(),
        P("sp", None, None),
    )
    out_specs = (
        P(("dp", "sp"), None, None),
        P("dp", "sp", None, None, None),
        P("dp", "sp", None, None),
    )
    return jax.shard_map(
        per_device, mesh=mesh, in_specs=in_specs, out_specs=out_specs, check_vma=False
    )
```

```python
import functools

import jax
import jax.numpy as jnp
from jax import lax
from jax.experimental import pallas as pl
from jax.experimental.pallas import tpu as pltpu
from jax.sharding import PartitionSpec as P

F32 = jnp.float32
BF16 = jnp.bfloat16
LEN = 128
DK = 128
DV = 128
CONV = 512
SLOTS = 32
SLOT_ROWS = 272
GROUP = 4
NLEVEL = 7
ORDER = (7, 5, 6, 3, 4, 1, 2, 0)
SMEM = pl.BlockSpec(memory_space=pltpu.SMEM)
VMEM = pl.BlockSpec(memory_space=pltpu.VMEM)
ANY = pl.BlockSpec(memory_space=pltpu.HBM)


def dot(lhs, rhs):
    return jnp.dot(lhs, rhs, preferred_element_type=F32)


def pack_kernel(info_ref, source_ref, state_ref, conv_ref, out_ref, slot_ref, src_scr):
    me = info_ref[0]

    def one_target(target, _):
        found = jnp.int32(0)
        for i in range(16):
            value = source_ref[target * 16 + i]
            src_scr[target * 2 + found] = value & 15
            found = jnp.minimum(found + jnp.where((value >> 4) == me, 1, 0), 2)
        return 0

    lax.fori_loop(0, 16, one_target, 0)

    def one_slot(slot, _):
        src = src_scr[slot] & 15
        for j in range(2):
            out_ref[slot, j * 128 : (j + 1) * 128, :] = state_ref[src, j].astype(BF16)
        out_ref[slot, 256:272, :] = conv_ref[src]
        return 0

    lax.fori_loop(0, SLOTS, one_slot, 0)

    for i in range(16):
        src_scr[i] = 0

    def one_wanted(i, _):
        origin = (source_ref[me * 16 + i] >> 4) & 15
        rank = jnp.minimum(src_scr[origin], 1)
        src_scr[origin] = rank + 1
        slot_ref[i] = origin * 2 + rank
        return 0

    lax.fori_loop(0, 16, one_wanted, 0)


def sigmoid(values):
    return 1.0 / (1.0 + jnp.exp(-values))


def delta_kernel(
    plan,
    first,
    unread,
    slots_ref,
    ids_ref,
    lengths_ref,
    dtb_ref,
    scale_ref,
    w_ref,
    wg_ref,
    convw_ref,
    gain_ref,
    *refs,
):
    size = min(GROUP, sum(n for _, n in plan))
    start_refs = refs[:size]
    x_refs = refs[size : size + len(plan)]
    refs = refs[size + len(plan) + unread :]
    core_ref, state_ref, tail_ref, seq_scr, z_scr, x_scr, state_scr, tail_scr = refs[:8]
    x_sem, state_sem, tail_sem = refs[8:]
    group = pl.program_id(0)
    rollouts = [ids_ref[first + group * size + i] for i in range(size)]
    lens = [lengths_ref[r] for r in rollouts]

    def x_copy(k):
        at, some = plan[k]
        rows = pl.ds(at * LEN, some * LEN)
        return pltpu.make_async_copy(x_refs[k], x_scr.at[rows], x_sem.at[k])

    @pl.when(group == 0)
    def _():
        for k in range(len(plan)):
            x_copy(k).start()

    steps = x_scr.shape[0] // LEN // size
    for step in range(steps):

        @pl.when(group == step)
        def _():
            for k in range(len(plan)):
                if plan[k][0] // size == step:
                    x_copy(k).wait()

    x_all = x_scr[pl.ds(group * size * LEN, size * LEN), :]
    gates_all = lax.dot_general(
        wg_ref[...], x_all, (((1,), (1,)), ((), ())), preferred_element_type=F32
    )[:8]
    for j in range(2):
        part = dot(x_all, w_ref[:, j * 256 : (j + 1) * 256]).astype(BF16).astype(F32)
        for i in range(size):
            seq_scr[i, 8 : 8 + LEN, j * 256 : (j + 1) * 256] = part[i * LEN : (i + 1) * LEN]
    z_scr[...] = dot(x_all, w_ref[:, 512:768]).astype(BF16)

    rows = lax.broadcasted_iota(jnp.int32, (LEN, LEN), 0)
    cols = lax.broadcasted_iota(jnp.int32, (LEN, LEN), 1)
    causal = rows >= cols
    strict = rows > cols
    ones_up = jnp.where(rows <= cols, 1.0, 0.0).astype(F32)
    levels = []
    for level in range(7):
        levels.append(
            ((rows >> (level + 1)) == (cols >> (level + 1)))
            & (((rows >> level) & 1) == 1)
            & (((cols >> level) & 1) == 0)
        )
    gain = gain_ref[...]
    line = lax.broadcasted_iota(jnp.int32, (8, LEN), 0)
    token = lax.broadcasted_iota(jnp.int32, (8, LEN), 1)
    bias = jnp.where(line == 2, dtb_ref[0, 0], dtb_ref[0, 1])
    scale = jnp.where(line == 2, -scale_ref[0, 0], -scale_ref[0, 1])

    chains = []
    per = []
    for i in range(size):
        conv_rows = start_refs[i][0, 256:272, :].astype(F32)
        for j in range(3):
            for c in range(4):
                seq_scr[i, 5 + j : 6 + j, c * 128 : (c + 1) * 128] = conv_rows[
                    j * 4 + c : j * 4 + c + 1, :
                ]
        acts = []
        for c in range(4):
            lanes = slice(c * 128, (c + 1) * 128)
            conv = convw_ref[0:1, lanes] * seq_scr[i, 5 : 5 + LEN, lanes]
            for j in range(1, 4):
                conv = conv + convw_ref[j : j + 1, lanes] * seq_scr[i, 5 + j : 5 + j + LEN, lanes]
            acts.append(conv * sigmoid(conv))
        query, key = acts[0], acts[1]
        query = query * (
            lax.rsqrt(jnp.sum(query * query, axis=-1, keepdims=True) + 1e-6) * DK ** (-0.5)
        )
        key = key * lax.rsqrt(jnp.sum(key * key, axis=-1, keepdims=True) + 1e-6)
        query = query.astype(BF16)
        key = key.astype(BF16)
        gates = gates_all[:, i * LEN : (i + 1) * LEN]
        alive = token < lens[i]
        beta = jnp.where(alive, sigmoid(gates), 0.0)
        shifted = gates + bias
        softplus = jnp.maximum(shifted, 0.0) + jnp.log1p(jnp.exp(-jnp.abs(shifted)))
        decay = jnp.where(alive, scale * softplus, 0.0)
        cum = jnp.dot(decay, ones_up, preferred_element_type=F32, precision=lax.Precision.HIGHEST)
        columns = jnp.where(line < 2, beta, cum).T
        key_t = key.T
        both = jnp.concatenate([key, query], axis=0)
        inner = dot(both, key_t)
        carry = jnp.concatenate([start_refs[i][0, 0:128, :], start_refs[i][0, 128:256, :]], axis=1)
        reads = dot(both, carry)
        per.append((key_t, cum, carry))
        for j in range(2):
            cum_col = columns[:, 2 + j : 3 + j]
            cum_row = cum[2 + j : 3 + j, :]
            beta_col = columns[:, j : j + 1]
            weight = jnp.exp(jnp.where(causal, cum_col - cum_row, -1e30))
            lower = jnp.where(strict, beta_col * weight * inner[:LEN], 0.0).astype(BF16)
            mixing = (weight * inner[LEN:]).astype(BF16)
            grow = jnp.exp(cum_col)
            target = beta_col * (acts[2 + j] - grow * reads[:LEN, j * 128 : (j + 1) * 128])
            chains.append(
                dict(
                    lower=lower,
                    mixing=mixing,
                    target=target.astype(BF16),
                    carried=grow * reads[LEN:, j * 128 : (j + 1) * 128],
                    last=jnp.exp(cum_row[:, LEN - 1 :] - cum_col),
                    inverse=jnp.where(rows == cols, 1.0, 0.0)
                    - jnp.where(levels[0], lower.astype(F32), 0.0),
                )
            )
    zero = jnp.zeros((), BF16)
    for level in range(1, NLEVEL):
        for ch in chains:
            inv = ch["inverse"].astype(BF16)
            step = dot(jnp.where(levels[level], ch["lower"], zero), inv)
            ch["inv"] = inv
            ch["step"] = step.astype(BF16)
        for ch in chains:
            ch["inverse"] = ch["inverse"] - dot(ch["inv"], ch["step"])
    for ch in chains:
        ch["update"] = dot(ch["inverse"].astype(BF16), ch["target"])
    for i in range(size):
        key_t, cum, carry = per[i]
        pair = chains[2 * i : 2 * i + 2]
        live = rows < lens[i]
        fresh = dot(
            key_t,
            jnp.concatenate([(ch["last"] * ch["update"]).astype(BF16) for ch in pair], axis=1),
        )
        for j, ch in enumerate(pair):
            lanes = slice(j * 128, (j + 1) * 128)
            keep = jnp.exp(cum[2 + j : 3 + j, LEN - 1 :])
            state_scr[group * size + i, j] = keep * carry[:, lanes].astype(F32) + fresh[:, lanes]
        for k in range(3):
            tail_scr[group * size + i, k : k + 1, :] = seq_scr[i, pl.ds(5 + k + lens[i], 1), :]
        tail_scr[group * size + i, 3:8, :] = jnp.zeros((5, CONV), F32)
        pltpu.make_async_copy(
            state_scr.at[group * size + i], state_ref.at[rollouts[i]], state_sem.at[group * size + i]
        ).start()
        pltpu.make_async_copy(
            tail_scr.at[group * size + i], tail_ref.at[rollouts[i]], tail_sem.at[group * size + i]
        ).start()
        for j, ch in enumerate(pair):
            lanes = slice(j * 128, (j + 1) * 128)
            read = ch["carried"] + dot(ch["mixing"], ch["update"].astype(BF16))
            inv_rms = lax.rsqrt(jnp.mean(read * read, axis=-1, keepdims=True) + 1e-6)
            z = z_scr[i * LEN : (i + 1) * LEN, lanes].astype(F32)
            core = jnp.where(live, read * inv_rms * gain * (z * sigmoid(z)), 0.0)
            core_ref[i if i < 2 else 5 - i, :, lanes] = core.astype(BF16)

    @pl.when(group == steps - 1)
    def _():
        for k in range(steps * size):
            r = ids_ref[first + k]
            pltpu.make_async_copy(state_scr.at[k], state_ref.at[r], state_sem.at[k]).wait()
            pltpu.make_async_copy(tail_scr.at[k], tail_ref.at[r], tail_sem.at[k]).wait()


def delta_call(scalars, arrays, arrived, pieces, plan, first, buffers, waits=()):
    count = sum(n for _, n in plan)
    size = min(GROUP, count)
    whole = lambda *shape: pl.BlockSpec(shape, lambda s, *_: (0,) * len(shape))
    start = [
        pl.BlockSpec(
            (1, SLOT_ROWS, 128), lambda s, slot, ids, *_, i=i: (slot[ids[first + s * size + i]], 0, 0)
        )
        for i in range(size)
    ]
    extra = list(buffers or ()) + list(waits)
    base = len(scalars) + len(arrays) + size + len(pieces)
    return pl.pallas_call(
        functools.partial(delta_kernel, plan, first, len(extra)),
        out_shape=[
            jax.ShapeDtypeStruct((count, LEN, 2 * DV), BF16),
            jax.ShapeDtypeStruct((16, 2, DK, DV), F32),
            jax.ShapeDtypeStruct((16, 8, CONV), F32),
        ],
        grid_spec=pltpu.PrefetchScalarGridSpec(
            num_scalar_prefetch=len(scalars),
            grid=(count // size,),
            in_specs=[whole(2048, 768), whole(16, 2048), whole(4, CONV), whole(1, DV)]
            + start
            + [ANY] * (len(pieces) + len(extra)),
            out_specs=[pl.BlockSpec((size, LEN, 2 * DV), lambda s, *_: (s, 0, 0)), ANY, ANY],
            scratch_shapes=[
                pltpu.VMEM((size, 144, CONV), F32),
                pltpu.VMEM((size * LEN, 2 * DV), BF16),
                pltpu.VMEM((count * LEN, 2048), BF16),
                pltpu.VMEM((count, 2, DK, DV), F32),
                pltpu.VMEM((count, 8, CONV), F32),
                pltpu.SemaphoreType.DMA((len(plan),)),
                pltpu.SemaphoreType.DMA((count,)),
                pltpu.SemaphoreType.DMA((count,)),
            ],
        ),
        input_output_aliases={base: 1, base + 1: 2} if buffers else {},
        compiler_params=pltpu.CompilerParams(vmem_limit_bytes=40 * 2**20),
        cost_estimate=pl.CostEstimate(
            flops=count * 1_250_000_000, bytes_accessed=count * 2**20, transcendentals=0
        ),
    )(*scalars, *arrays, *[arrived] * size, *pieces, *extra)


def project_kernel(info_ref, w_ref, *refs):
    core_refs = refs[:8]
    own_ref, other_ref, w_scr, row_scr, sems = refs[8:]
    copies = []
    for q in range(4):
        some = pl.ds(4 * q, 4)
        copy = pltpu.make_async_copy(w_ref.at[some], w_scr.at[some], sems.at[q])
        copy.start()
        copies.append(copy)
    for d in range(8):
        spot = info_ref[4 + d]
        row_scr[spot] = core_refs[d][...].reshape(2 * LEN, 2 * DV)
    lhs = jnp.concatenate([row_scr[i] for i in range(8)], axis=1)
    for q in range(4):
        copies[q].wait()
        for n in range(2):
            at = 4 * q + 2 * n
            rhs = [w_scr[at + k].reshape(8 * 256, 128) for k in range(2)]
            acc = dot(lhs, jnp.concatenate(rhs, axis=1))
            lanes = slice(q * 512 + n * 256, q * 512 + (n + 1) * 256)
            own_ref[:, lanes] = acc[:LEN].astype(BF16)
            other_ref[:, lanes] = acc[LEN:].astype(BF16)


def project_call(info, weights, cores):
    return pl.pallas_call(
        project_kernel,
        out_shape=[
            jax.ShapeDtypeStruct((LEN, 2048), BF16),
            jax.ShapeDtypeStruct((LEN, 2048), BF16),
        ],
        in_specs=[SMEM, ANY] + [VMEM] * 8,
        out_specs=[VMEM] * 2,
        scratch_shapes=[
            pltpu.VMEM((16, 8, 256, 128), BF16),
            pltpu.VMEM((8, 2 * LEN, 256), BF16),
            pltpu.SemaphoreType.DMA((4,)),
        ],
        compiler_params=pltpu.CompilerParams(vmem_limit_bytes=58 * 2**20),
        cost_estimate=pl.CostEstimate(
            flops=2 * 256 * 2048 * 128 * 16, bytes_accessed=10 * 2**20, transcendentals=0
        ),
    )(info, weights, *cores)


SWAP = [(i, i ^ 1) for i in range(16)]


def along(shift):
    return [(2 * z + c, 2 * ((z + (shift if c == 0 else -shift)) % 8) + c) for z in range(8) for c in range(2)]


def move(values, shift):
    return lax.ppermute(values, "sp", along(shift))


def swap(values):
    return lax.ppermute(values, "sp", SWAP)


def after(value, *others):
    return lax.optimization_barrier((value, *others))[0]


def per_device(
    hidden,
    lengths,
    source_slot,
    old_state,
    old_conv,
    w_in,
    w_gates,
    conv_weight,
    decay_scale,
    dt_bias,
    norm_gain,
    w_out,
):
    owner = lax.axis_index("dp")
    place = lax.axis_index("sp")
    level, core = place // 2, place % 2
    way = 1 - 2 * core
    zs, ids = [level], []
    for step in (1, 2, 3):
        for sign in (-1, 1):
            zs.append((level + sign * step * way) % 8)
            ids += [2 * zs[-1] + core, 2 * zs[-1] + 1 - core][::-sign]
    zs.append((level + 4) % 8)
    for chip in (zs[-1], level):
        ids += [2 * chip + core, 2 * chip + 1 - core]
    info = jnp.stack([owner, level, core, owner] + zs).astype(jnp.int32)
    ids = jnp.stack(ids).astype(jnp.int32)

    own = hidden[0]
    s0 = swap(own)

    conv_rows = jnp.pad(old_conv[:, 0].reshape(16, 12, 128), ((0, 0), (0, 4), (0, 0)))
    packed, slots = pl.pallas_call(
        pack_kernel,
        out_shape=[
            jax.ShapeDtypeStruct((SLOTS, SLOT_ROWS, 128), BF16),
            jax.ShapeDtypeStruct((16,), jnp.int32),
        ],
        in_specs=[SMEM, SMEM, VMEM, VMEM],
        out_specs=[VMEM, SMEM],
        scratch_shapes=[pltpu.SMEM((40,), jnp.int32)],
        compiler_params=pltpu.CompilerParams(vmem_limit_bytes=24 * 2**20),
    )(info, source_slot, old_state[:, 0], conv_rows)
    arrived = lax.all_to_all(packed, "dp", split_axis=0, concat_axis=0, tiled=True)

    held0 = jnp.concatenate([own, after(s0, packed)], axis=0)
    ring1 = move(held0, 1)
    arrived = after(arrived, ring1)
    held1 = after(ring1, arrived)
    ring2, w1 = move(held1, 1), swap(held1)

    share = lax.dynamic_slice_in_dim(w_out[0], owner // 2 * 256, 256, 1)
    spread = after(lax.all_gather(share, "sp", axis=0, tiled=False), held1)
    heads = lax.dynamic_slice(
        spread.reshape(8, 2, 256, 256), (0, core, 0, owner % 2 * 128), (8, 1, 256, 128)
    )[:, 0]
    weights = lax.all_gather(heads, "dp", axis=0, tiled=False)

    gates = jnp.pad(w_gates[:, 0].T, ((0, 12), (0, 0)))
    scalars = (slots, ids, lengths, dt_bias, decay_scale)
    arrays = (w_in[:, 0], gates, conv_weight[0], norm_gain[None])
    cores = [None] * 8
    plan = ((0, 2), (2, 2))
    done, *buffers = delta_call(scalars, arrays, arrived, (held1, w1), plan, 0, None, (spread,))
    held2 = after(ring2, done)
    ring3, w2 = move(held2, 1), swap(held2)
    cores[2], cores[1] = move(done[0:2], -1), move(done[2:4], 1)
    done, *buffers = delta_call(scalars, arrays, arrived, (held2, w2), plan, 4, buffers)
    cores[4], cores[3] = move(done[0:2], -2), move(done[2:4], 2)
    done, *buffers = delta_call(scalars, arrays, arrived, (held0,), ((0, 2),), 14, buffers)
    cores[0] = done
    held3 = after(ring3, done, cores[1], cores[2])
    ring4, w3 = move(held3[:LEN], 1), swap(held3)
    done, *buffers = delta_call(scalars, arrays, arrived, (held3, w3), plan, 8, buffers)
    cores[6], cores[5] = move(done[0:2], -3), move(done[2:4], 3)
    ring4 = after(ring4, done, cores[3], cores[4])
    plan = ((0, 1), (1, 1))
    done, *buffers = delta_call(scalars, arrays, arrived, (ring4, swap(ring4)), plan, 12, buffers)
    cores[7] = move(done, 4)
    new_state, tails = buffers
    new_conv = tails[:, :3].astype(BF16)
    cores[0], new_conv = lax.optimization_barrier((cores[0], new_conv))
    mine, theirs = project_call(info, weights, cores)
    layer_out = (mine.astype(F32) + swap(theirs).astype(F32)).astype(BF16)
    return layer_out[None], new_state[:, None], new_conv[:, None]


def solution(mesh):
    in_specs = (
        P(("dp", "sp"), None, None),
        P("dp"),
        P(),
        P("dp", "sp", None, None, None),
        P("dp", "sp", None, None),
        P(None, "sp", None),
        P(None, "sp", None),
        P("sp", None, None),
        P("sp", None),
        P("sp", None),
        P(),
        P("sp", None, None),
    )
    out_specs = (
        P(("dp", "sp"), None, None),
        P("dp", "sp", None, None, None),
        P("dp", "sp", None, None),
    )
    return jax.shard_map(
        per_device, mesh=mesh, in_specs=in_specs, out_specs=out_specs, check_vma=False
    )
```
